256 devices in a mesh: depth: 2 (over core), row: 16 (over y, x), col: 8 (over z).
Axes of the slice: x: 4, y: 4, z: 8, core: 2. Of those that a mesh axis runs over, the one named last changes fastest.
Arguments:
- inputs: bfloat16 [256, 12288], P(('depth', 'col'), 'row'), may hold values from -6 to 6
- up_blocks: bfloat16 [16, 8, 108, 128, 128], P('row', 'col'), may hold values from -0.109375 to 0.109375
- down_blocks: bfloat16 [16, 8, 108, 128, 128], P('row', 'col'), may hold values from -0.0546875 to 0.0546875
- slots: int32 [16, 8, 108], P('row', 'col'), may hold values from 0 to 287, as said below
- counts: int32 [16, 8], P('row', 'col'), may hold values from 27 to 108, as said below
- grad_out: bfloat16 [256, 12288], P(('depth', 'col'), 'row'), may hold values from -6 to 6
Outputs:
- outputs: bfloat16 [256, 12288], P(('depth', 'col'), 'row')
- grad_in: bfloat16 [256, 12288], P(('depth', 'col'), 'row')
- grad_up: bfloat16 [16, 8, 108, 128, 128], P('row', 'col', 'depth')
- grad_down: bfloat16 [16, 8, 108, 128, 128], P('row', 'col', 'depth')
The draws below stay inside these ranges and needn't reach their ends.
Inputs may be any that keep to these rules, and one draw needn't show every extreme that they name: `slots`: within each tile the 108 slot numbers are distinct local block numbers of 0 to 287. `counts`: some tile is full and some tile has the fewest live slots.
All inputs are finite; a program needn't handle non-finite values.
Results may differ from the reference program's by a relative error of at most 0.0059.
Values may be sent and summed in bfloat16 or wider, within the bound.
A program may use at most 128 MiB of HBM per device.

```python
import jax
import jax.numpy as jnp

D = 12288
FF = 49152
BLK = 128
TOKENS = 256
D_BLOCKS = 6
F_BLOCKS = 48
CAP = 108
N_DEPTH = 2
N_ROW = 16
N_COL = 8


def draw_slots(key, part):
    key = jax.random.fold_in(key, 11)
    tile_keys = jax.random.split(key, N_ROW * N_COL)

    def one_tile(tile_key):
        return jax.random.permutation(tile_key, D_BLOCKS * F_BLOCKS)[:CAP]
    picked = jax.vmap(one_tile)(tile_keys)
    return picked.reshape(N_ROW, N_COL, CAP).astype(jnp.int32)


def draw_counts(key, part):
    key = jax.random.fold_in(key, 12)
    key_one, key_two, key_three = jax.random.split(key, 3)
    tile_total = N_ROW * N_COL
    drawn = jax.random.randint(key_one, (tile_total,), CAP // 4, CAP + 1)
    top_tile = jax.random.randint(key_two, (), 0, tile_total)
    low_tile = (top_tile + 1 + jax.random.randint(key_three, (), 0, tile_total - 1)) % tile_total
    places = jnp.arange(tile_total)
    drawn = jnp.where(places == top_tile, CAP, jnp.where(places == low_tile, CAP // 4, drawn))
    return drawn.reshape(N_ROW, N_COL).astype(jnp.int32)


def steps_of(key, extent, shards, smallest, top_value):
    level, own = 1.0, jax.random.fold_in(key, 6)
    for dim, blocks in shards:
        steps = jnp.exp(jax.random.uniform(jax.random.fold_in(own, dim), (blocks,), jnp.float32, smallest / len(shards), top_value / len(shards)))
        level = level * jnp.repeat(steps, extent[dim] // blocks).reshape([-1 if axis == dim else 1 for axis in range(len(extent))])
    return level


def centred(key, extent, spread, reach, shards=(), dtype=jnp.bfloat16):
    entries = jax.random.normal(key, extent, jnp.float32) * spread
    if len(shards) > 0:
        entries = steps_of(key, extent, shards, -0.22, 0.18) * entries
    return jnp.clip(entries, min=-reach, max=reach).astype(dtype)


def setup_inputs(seed: int = 0) -> dict:
    seeds = jax.random.split(jax.random.key(seed), 7)
    inputs = centred(seeds[0], (TOKENS, D), 1.0, 6.0, ((0, 16), (1, 16)))
    up_blocks = centred(seeds[1], (N_ROW, N_COL, CAP, BLK, BLK), (D // 4) ** -0.5, 0.109375, ((0, 16), (1, 8)))
    down_blocks = centred(seeds[2], (N_ROW, N_COL, CAP, BLK, BLK), (FF // 4) ** -0.5, 0.0546875, ((0, 16), (1, 8)))
    slots = draw_slots(jax.random.fold_in(seeds[6], 71), 0)
    counts = draw_counts(jax.random.fold_in(seeds[6], 71), 0)
    grad_out = centred(seeds[5], (TOKENS, D), 1.0, 6.0, ((0, 16), (1, 16)))
    return dict(inputs=inputs, up_blocks=up_blocks, down_blocks=down_blocks, slots=slots, counts=counts, grad_out=grad_out)


root_coeff = 0.7978845608
cube_coeff = 0.044715


def gelu_parts(preact):
    cubed = preact * preact * preact
    tangent = jnp.tanh(root_coeff * (preact + cube_coeff * cubed))
    values = 0.5 * preact * (1.0 + tangent)
    slopes = 0.5 * (1.0 + tangent) + 0.5 * preact * (1.0 - tangent * tangent) * root_coeff * (1.0 + 3.0 * cube_coeff * preact * preact)
    return values, slopes


def pick_blocks(rows_in, block_ids, block_size):
    height = rows_in.shape[0]
    return rows_in.reshape(height, -1, block_size)[:, block_ids, :]


def spread_blocks(products, block_ids, block_count):
    height, slot_count, block_size = products.shape
    moved = jnp.transpose(products, (1, 0, 2))
    summed = jax.ops.segment_sum(moved, block_ids, num_segments=block_count)
    return jnp.transpose(summed, (1, 0, 2)).reshape(height, block_count * block_size)


def reference(inputs, up_blocks, down_blocks, slots, counts, grad_out):
    width_tile = D // N_ROW
    hidden_tile = FF // N_COL
    half_rows = TOKENS // N_DEPTH
    x_full = inputs.astype(jnp.float32)
    g_full = grad_out.astype(jnp.float32)
    tiles = {}
    for r_index in range(N_ROW):
        for c_index in range(N_COL):
            alive_mask = (jnp.arange(CAP) < counts[r_index, c_index]).astype(jnp.float32)
            block_in = (slots[r_index, c_index] // F_BLOCKS).astype(jnp.int32)
            block_out = (slots[r_index, c_index] % F_BLOCKS).astype(jnp.int32)
            weight_one = up_blocks[r_index, c_index].astype(jnp.float32) * alive_mask[:, None, None]
            weight_two = down_blocks[r_index, c_index].astype(jnp.float32) * alive_mask[:, None, None]
            tiles[(r_index, c_index)] = (alive_mask, block_in, block_out, weight_one, weight_two)
    pre_cols = []
    for c_index in range(N_COL):
        accum = jnp.zeros((TOKENS, hidden_tile), jnp.float32)
        for r_index in range(N_ROW):
            alive_mask, block_in, block_out, weight_one, weight_two = tiles[(r_index, c_index)]
            chosen = pick_blocks(x_full[:, r_index * width_tile:(r_index + 1) * width_tile], block_in, BLK)
            accum = accum + spread_blocks(jnp.einsum('tsa,sab->tsb', chosen, weight_one), block_out, F_BLOCKS)
        pre_cols.append(accum)
    preact = jnp.concatenate(pre_cols, axis=1)
    values, slopes = gelu_parts(preact)
    hidden = values.astype(jnp.bfloat16)
    hidden_full = hidden.astype(jnp.float32)
    grad_cols = []
    for c_index in range(N_COL):
        accum = jnp.zeros((TOKENS, hidden_tile), jnp.float32)
        for r_index in range(N_ROW):
            alive_mask, block_in, block_out, weight_one, weight_two = tiles[(r_index, c_index)]
            chosen = pick_blocks(g_full[:, r_index * width_tile:(r_index + 1) * width_tile], block_in, BLK)
            accum = accum + spread_blocks(jnp.einsum('tsa,sba->tsb', chosen, weight_two), block_out, F_BLOCKS)
        grad_cols.append(accum)
    grad_hidden = jnp.concatenate(grad_cols, axis=1)
    grad_pre = (grad_hidden * slopes).astype(jnp.bfloat16)
    grad_pre_full = grad_pre.astype(jnp.float32)
    out_cols = []
    din_cols = []
    for r_index in range(N_ROW):
        out_acc = jnp.zeros((TOKENS, width_tile), jnp.float32)
        din_acc = jnp.zeros((TOKENS, width_tile), jnp.float32)
        for c_index in range(N_COL):
            alive_mask, block_in, block_out, weight_one, weight_two = tiles[(r_index, c_index)]
            hid_slice = hidden_full[:, c_index * hidden_tile:(c_index + 1) * hidden_tile]
            gp_slice = grad_pre_full[:, c_index * hidden_tile:(c_index + 1) * hidden_tile]
            out_acc = out_acc + spread_blocks(jnp.einsum('tsb,sba->tsa', pick_blocks(hid_slice, block_out, BLK), weight_two), block_in, D_BLOCKS)
            din_acc = din_acc + spread_blocks(jnp.einsum('tsb,sab->tsa', pick_blocks(gp_slice, block_out, BLK), weight_one), block_in, D_BLOCKS)
        out_cols.append(out_acc)
        din_cols.append(din_acc)
    outputs = jnp.concatenate(out_cols, axis=1).astype(jnp.bfloat16)
    grad_in = jnp.concatenate(din_cols, axis=1).astype(jnp.bfloat16)
    up_rows = []
    down_rows = []
    for r_index in range(N_ROW):
        up_tiles = []
        down_tiles = []
        for c_index in range(N_COL):
            alive_mask, block_in, block_out, weight_one, weight_two = tiles[(r_index, c_index)]
            up_sum = jnp.zeros((CAP, BLK, BLK), jnp.float32)
            down_sum = jnp.zeros((CAP, BLK, BLK), jnp.float32)
            for d_index in range(N_DEPTH):
                low = d_index * half_rows
                high = low + half_rows
                x_part = pick_blocks(x_full[low:high, r_index * width_tile:(r_index + 1) * width_tile], block_in, BLK)
                g_part = pick_blocks(g_full[low:high, r_index * width_tile:(r_index + 1) * width_tile], block_in, BLK)
                h_part = pick_blocks(hidden_full[low:high, c_index * hidden_tile:(c_index + 1) * hidden_tile], block_out, BLK)
                p_part = pick_blocks(grad_pre_full[low:high, c_index * hidden_tile:(c_index + 1) * hidden_tile], block_out, BLK)
                part_up = (jnp.einsum('tsa,tsb->sab', x_part, p_part) * alive_mask[:, None, None]).astype(jnp.bfloat16)
                part_down = (jnp.einsum('tsb,tsa->sba', h_part, g_part) * alive_mask[:, None, None]).astype(jnp.bfloat16)
                up_sum = up_sum + part_up.astype(jnp.float32)
                down_sum = down_sum + part_down.astype(jnp.float32)
            up_tiles.append(up_sum.astype(jnp.bfloat16))
            down_tiles.append(down_sum.astype(jnp.bfloat16))
        up_rows.append(jnp.stack(up_tiles))
        down_rows.append(jnp.stack(down_tiles))
    grad_up = jnp.stack(up_rows)
    grad_down = jnp.stack(down_rows)
    return (outputs, grad_in, grad_up, grad_down)
```

```python
import jax
import jax.numpy as jnp
from jax import lax
from jax.experimental import pallas as pl
from jax.experimental.pallas import tpu as pltpu
from jax.sharding import PartitionSpec as P

MESH = pl.DeviceIdType.MESH
F32, BF16 = jnp.float32, jnp.bfloat16
BLK, CAP, HALF = 128, 108, 54
WB, FB = 6, 48
NX, NY, NZ = 4, 4, 8
CHUNKS = 3
ROWS = 16

root_coeff = 0.7978845608
cube_coeff = 0.044715


def gelu_parts(preact):
    cubed = preact * preact * preact
    tangent = jnp.tanh(root_coeff * (preact + cube_coeff * cubed))
    values = 0.5 * preact * (1.0 + tangent)
    slopes = 0.5 * (1.0 + tangent) + 0.5 * preact * (1.0 - tangent * tangent) * root_coeff * (
        1.0 + 3.0 * cube_coeff * preact * preact
    )
    return (values, slopes)


def dot(a, b):
    return lax.dot_general(a, b, (((1,), (0,)), ((), ())), preferred_element_type=F32)


def dot_t(a, b):
    return lax.dot_general(a, b, (((1,), (1,)), ((), ())), preferred_element_type=F32)


def quad(a, b, c, d):
    return jnp.concatenate(
        [jnp.concatenate([a, b], axis=1), jnp.concatenate([c, d], axis=1)], axis=0
    )


def kernel(
    inv, slots, counts, x_in, g_in, up_in, dn_in,
    out_ref, gin_ref, gup_ref, gdn_ref,
    up, dn, xs, gs, xt, gt, pbuf, gbuf, r1p, r1g, s2p, s2g, ownp, owng, r2p, r2g,
    hid, pre, acc_o, acc_i, send_o, send_i, recv_o, recv_i, gup_v, gdn_v,
    wsem, lsem, ssem_a, rsem_a, ssem_1, rsem_1, ssem_2, rsem_2, ssem_h, rsem_h, ssem_q, rsem_q,
    ssem_d, rsem_d, ssem_z, rsem_z, osem,
):
    d, r, c = lax.axis_index("depth"), lax.axis_index("row"), lax.axis_index("col")
    y, x = r // NX, r % NX
    sends = []

    def at_x(o):
        return (d, y * NX + (x + o) % NX, c)

    def at_y(o):
        return (d, ((y + o) % NY) * NX + x, c)

    def at_z(o):
        return (d, r, (c + o) % NZ)

    partner = (1 - d, r, c)

    def remote(src, dst, ssem, rsem, device):
        copy = pltpu.make_async_remote_copy(
            src_ref=src, dst_ref=dst, send_sem=ssem, recv_sem=rsem, device_id=device, device_id_type=MESH
        )
        copy.start()
        sends.append(copy)
        return copy

    load_up = pltpu.make_async_copy(up_in.at[0, 0], up.at[pl.ds(0, CAP)], wsem.at[0])
    load_dn = pltpu.make_async_copy(dn_in.at[0, 0], dn.at[pl.ds(0, CAP)], wsem.at[1])
    mine = pl.ds(pl.multiple_of(c * ROWS, ROWS), ROWS)
    load_x = pltpu.make_async_copy(x_in, xs.at[0, mine], lsem.at[0])
    load_g = pltpu.make_async_copy(g_in, gs.at[0, mine], lsem.at[1])
    load_x.start()
    load_g.start()
    load_up.start()
    load_dn.start()
    up[CAP] = jnp.zeros((BLK, BLK), BF16)
    dn[CAP] = jnp.zeros((BLK, BLK), BF16)

    barrier = pltpu.get_barrier_semaphore()
    peers = [at_x(o) for o in (1, 2, 3)] + [at_y(o) for o in (1, 2, 3)]
    peers += [at_z(o) for o in range(1, NZ)] + [partner]
    for peer in peers:
        pl.semaphore_signal(barrier, inc=1, device_id=peer, device_id_type=MESH)
    pl.semaphore_wait(barrier, len(peers))

    far_first = (4, 3, 5, 2, 6, 1, 7)
    got_x, got_g = [], []
    for n, (src, dst, got) in enumerate(((x_in, xs, got_x), (g_in, gs, got_g))):
        for o in far_first:
            got.append(remote(src, dst.at[0, mine], ssem_a.at[n, o - 1], rsem_a.at[n, o - 1], at_z(o)))

    def block(weights, i, f):
        return weights[inv[i * FB + f]]

    def pair_p(fa, fb):
        acc = None
        for kk in range(3):
            w = quad(block(up, 2 * kk, fa), block(up, 2 * kk, fb), block(up, 2 * kk + 1, fa), block(up, 2 * kk + 1, fb))
            term = dot(xs[0, :, 256 * kk : 256 * kk + 256], w)
            acc = term if acc is None else acc + term
        return acc

    def pair_g(fa, fb):
        acc = None
        for kk in range(3):
            w = quad(block(dn, 2 * kk, fa), block(dn, 2 * kk + 1, fa), block(dn, 2 * kk, fb), block(dn, 2 * kk + 1, fb))
            term = dot_t(gs[0, :, 256 * kk : 256 * kk + 256], w)
            acc = term if acc is None else acc + term
        return acc

    got_1p, got_1g, got_2p, got_2g = {}, {}, {}, {}

    def make_p(k):
        for o in (2, 1, 3, 0):
            xx = (x + o) % NX

            def body(m, carry, xx=xx):
                fa = 16 * k + 8 * m + xx
                acc = pair_p(fa, fa + NX).astype(BF16)
                pbuf[k, xx * 4 + 2 * m] = acc[:, :BLK]
                pbuf[k, xx * 4 + 2 * m + 1] = acc[:, BLK:]
                return carry

            lax.fori_loop(0, 2, body, 0)
            if o:
                got_1p[k, o] = remote(
                    pbuf.at[k, pl.ds(xx * 4, 4)], r1p.at[k, o - 1], ssem_1.at[0, k, o - 1], rsem_1.at[0, k, o - 1], at_x(o)
                )

    def make_g(k):
        for o in (2, 1, 3, 0):
            yy = (y + o) % NY

            def body(m, carry, yy=yy):
                fa = 16 * k + 4 * yy + 2 * m
                acc = pair_g(fa, fa + 1).astype(BF16)
                gbuf[k, yy * 4 + 2 * m] = acc[:, :BLK]
                gbuf[k, yy * 4 + 2 * m + 1] = acc[:, BLK:]
                return carry

            lax.fori_loop(0, 2, body, 0)
            if o:
                got_1g[k, o] = remote(
                    gbuf.at[k, pl.ds(yy * 4, 4)], r1g.at[k, o - 1], ssem_1.at[1, k, o - 1], rsem_1.at[1, k, o - 1], at_y(o)
                )

    def second(k, n, buf, base, here, r1, s2, own, r2, got_1, got_2, at):
        for o in (1, 2, 3):
            got_1[k, o].wait_recv()
        for o in (2, 1, 3, 0):
            p = (here + o) % 4
            total = buf[k, base * 4 + p].astype(F32)
            for j in range(3):
                total = total + r1[k, j, p].astype(F32)
            if o:
                s2[k, p] = total.astype(BF16)
                got_2[k, o] = remote(s2.at[k, p], r2.at[k, o - 1], ssem_2.at[n, k, o - 1], rsem_2.at[n, k, o - 1], at(o))
            else:
                own[k] = total

    def second_p(k):
        second(k, 0, pbuf, x, y, r1p, s2p, ownp, r2p, got_1p, got_2p, at_y)

    def second_g(k):
        second(k, 1, gbuf, y, x, r1g, s2g, owng, r2g, got_1g, got_2g, at_x)

    got_h1, got_h2, got_q1, got_q2, got_d = {}, {}, {}, {}, {}
    hpos, qpos = x * 4 + y, y * 4 + x

    def activate(k):
        for o in (1, 2, 3):
            got_2p[k, o].wait_recv()
        p = ownp[k]
        for j in range(3):
            p = p + r2p[k, j].astype(F32)
        values, slopes = gelu_parts(p)
        hid[0, k, hpos] = values.astype(BF16)
        for o in (2, 1, 3):
            spot = hid.at[0, k, hpos]
            got_h1[k, o] = remote(spot, spot, ssem_h.at[0, k, o - 1], rsem_h.at[0, k, o - 1], at_y(o))
        for o in (1, 2, 3):
            got_2g[k, o].wait_recv()
        g = owng[k]
        for j in range(3):
            g = g + r2g[k, j].astype(F32)
        pre[0, k, qpos] = (g * slopes).astype(BF16)
        for o in (2, 1, 3):
            spot = pre.at[0, k, qpos]
            got_q1[k, o] = remote(spot, spot, ssem_q.at[0, k, o - 1], rsem_q.at[0, k, o - 1], at_x(o))

    def spread(k):
        for o in (1, 2, 3):
            got_h1[k, o].wait_recv()
        for o in (2, 1, 3):
            spot = hid.at[0, k, pl.ds(x * 4, 4)]
            got_h2[k, o] = remote(spot, spot, ssem_h.at[1, k, o - 1], rsem_h.at[1, k, o - 1], at_x(o))
        for o in (1, 2, 3):
            got_q1[k, o].wait_recv()
        for o in (2, 1, 3):
            spot = pre.at[0, k, pl.ds(y * 4, 4)]
            got_q2[k, o] = remote(spot, spot, ssem_q.at[1, k, o - 1], rsem_q.at[1, k, o - 1], at_y(o))

    def use_h(k):
        for o in (1, 2, 3):
            got_h2[k, o].wait_recv()
        got_d[0, k] = remote(hid.at[0, k], hid.at[1, k], ssem_d.at[0, k], rsem_d.at[0, k], partner)
        for n in range(3):

            def body(p, acc, n=n):
                xx, m = p // 2, p % 2
                fa = 16 * k + 8 * m + xx
                fb = fa + 4
                h = jnp.concatenate([hid[0, k, xx * 4 + 2 * m], hid[0, k, xx * 4 + 2 * m + 1]], axis=1)
                w = quad(block(dn, 2 * n, fa), block(dn, 2 * n + 1, fa), block(dn, 2 * n, fb), block(dn, 2 * n + 1, fb))
                return acc + dot(h, w)

            cols = slice(256 * n, 256 * n + 256)
            start = jnp.zeros((BLK, 256), F32) if k == 0 else acc_o[:, cols]
            acc_o[:, cols] = lax.fori_loop(0, 8, body, start)

    def use_q(k):
        for o in (1, 2, 3):
            got_q2[k, o].wait_recv()
        got_d[1, k] = remote(pre.at[0, k], pre.at[1, k], ssem_d.at[1, k], rsem_d.at[1, k], partner)
        for n in range(3):

            def body(p, acc, n=n):
                fa = 16 * k + 2 * p
                fb = fa + 1
                q = jnp.concatenate([pre[0, k, 2 * p], pre[0, k, 2 * p + 1]], axis=1)
                w = quad(block(up, 2 * n, fa), block(up, 2 * n, fb), block(up, 2 * n + 1, fa), block(up, 2 * n + 1, fb))
                return acc + dot_t(q, w)

            cols = slice(256 * n, 256 * n + 256)
            start = jnp.zeros((BLK, 256), F32) if k == 0 else acc_i[:, cols]
            acc_i[:, cols] = lax.fori_loop(0, 8, body, start)

    def scatter(n, acc, buf, recv):
        got = []
        buf[...] = acc[...].astype(BF16)
        for o in far_first:
            cc = (c + o) % NZ
            rows = pl.ds(pl.multiple_of(cc * ROWS, ROWS), ROWS)
            got.append(remote(buf.at[rows], recv.at[o - 1], ssem_z.at[n, o - 1], rsem_z.at[n, o - 1], at_z(o)))
        return got

    def gather_up(got, acc, recv, result):
        for copy in got:
            copy.wait_recv()
        total = acc[mine, :]
        for j in range(NZ - 1):
            total = total + recv[j].astype(F32)
        result[...] = total.astype(BF16)

    load_x.wait()
    for copy in got_x:
        copy.wait_recv()
    load_up.wait()
    make_p(0)
    load_g.wait()
    for copy in got_g:
        copy.wait_recv()
    load_dn.wait()
    make_g(0)
    got_d["x"] = remote(xs.at[0], xs.at[1], ssem_d.at[2, 0], rsem_d.at[2, 0], partner)
    got_d["g"] = remote(gs.at[0], gs.at[1], ssem_d.at[2, 1], rsem_d.at[2, 1], partner)
    make_p(1)
    second_p(0)
    make_g(1)
    second_g(0)
    make_p(2)
    second_p(1)
    activate(0)
    make_g(2)
    second_g(1)
    spread(0)
    second_p(2)
    activate(1)
    second_g(2)
    spread(1)
    use_h(0)
    use_q(0)
    activate(2)
    spread(2)
    use_h(1)
    use_q(1)
    got_d["x"].wait_recv()
    got_d["g"].wait_recv()
    for i in range(WB):
        cols = slice(BLK * i, BLK * i + BLK)
        for half in range(2):
            xt[i, :, BLK * half : BLK * half + BLK] = xs[half, :, cols].T
            gt[i, half] = gs[half, :, cols]
    use_h(2)
    got_o = scatter(0, acc_o, send_o, recv_o)
    use_q(2)
    got_i = scatter(1, acc_i, send_i, recv_i)

    alive = counts[0, 0]

    def grad_down(s, carry):
        slot = d * HALF + s
        number = slots[0, 0, slot]
        i, f = number // FB, number % FB
        k, yy, xx = f // 16, (f % 16) // 4, f % 4
        hpair = jnp.concatenate([hid[0, k, xx * 4 + yy], hid[1, k, xx * 4 + yy]], axis=0)
        gpair = jnp.concatenate([gt[i, 0], gt[i, 1]], axis=0)
        part = lax.dot_general(hpair, gpair, (((0,), (0,)), ((), ())), preferred_element_type=F32)
        live = jnp.where(slot < alive, 1.0, 0.0)
        gdn_v[s] = (part * live).astype(BF16)
        return carry

    def grad_up(s, carry):
        slot = d * HALF + s
        number = slots[0, 0, slot]
        i, f = number // FB, number % FB
        k, yy, xx = f // 16, (f % 16) // 4, f % 4
        qpair = jnp.concatenate([pre[0, k, yy * 4 + xx], pre[1, k, yy * 4 + xx]], axis=0)
        part = dot(xt[i], qpair)
        live = jnp.where(slot < alive, 1.0, 0.0)
        gup_v[s] = (part * live).astype(BF16)
        return carry

    stores = []

    def write(n, body, held, result):
        for part in range(3):
            lax.fori_loop(18 * part, 18 * part + 18, body, 0)
            span = pl.ds(18 * part, 18)
            copy = pltpu.make_async_copy(held.at[span], result.at[0, 0, span], osem.at[n, part])
            copy.start()
            stores.append(copy)

    for k in range(CHUNKS):
        got_d[0, k].wait_recv()
    write(0, grad_down, gdn_v, gdn_ref)
    gather_up(got_o, acc_o, recv_o, out_ref)
    for k in range(CHUNKS):
        got_d[1, k].wait_recv()
    write(1, grad_up, gup_v, gup_ref)
    gather_up(got_i, acc_i, recv_i, gin_ref)
    for copy in sends:
        copy.wait_send()
    for copy in stores:
        copy.wait()


def on_device(inputs, up_blocks, down_blocks, slots, counts, grad_out):
    places = jnp.arange(WB * FB, dtype=jnp.int32)
    order = jnp.arange(CAP, dtype=jnp.int32)
    held = (slots[0, 0][None, :] == places[:, None]) & (order < counts[0, 0])[None, :]
    inv = jnp.min(jnp.where(held, order[None, :], CAP), axis=1)
    smem = pl.BlockSpec(memory_space=pltpu.SMEM)
    vmem = pl.BlockSpec(memory_space=pltpu.VMEM)
    anym = pl.BlockSpec(memory_space=pl.ANY)
    dma = pltpu.SemaphoreType.DMA
    scratch = [
        pltpu.VMEM((CAP + 1, BLK, BLK), BF16),
        pltpu.VMEM((CAP + 1, BLK, BLK), BF16),
        pltpu.VMEM((2, BLK, WB * BLK), BF16),
        pltpu.VMEM((2, BLK, WB * BLK), BF16),
        pltpu.VMEM((WB, BLK, 2 * BLK), BF16),
        pltpu.VMEM((WB, 2, BLK, BLK), BF16),
        pltpu.VMEM((CHUNKS, 16, BLK, BLK), BF16),
        pltpu.VMEM((CHUNKS, 16, BLK, BLK), BF16),
        pltpu.VMEM((CHUNKS, 3, 4, BLK, BLK), BF16),
        pltpu.VMEM((CHUNKS, 3, 4, BLK, BLK), BF16),
        pltpu.VMEM((CHUNKS, 4, BLK, BLK), BF16),
        pltpu.VMEM((CHUNKS, 4, BLK, BLK), BF16),
        pltpu.VMEM((CHUNKS, BLK, BLK), F32),
        pltpu.VMEM((CHUNKS, BLK, BLK), F32),
        pltpu.VMEM((CHUNKS, 3, BLK, BLK), BF16),
        pltpu.VMEM((CHUNKS, 3, BLK, BLK), BF16),
        pltpu.VMEM((2, CHUNKS, 16, BLK, BLK), BF16),
        pltpu.VMEM((2, CHUNKS, 16, BLK, BLK), BF16),
        pltpu.VMEM((BLK, WB * BLK), F32),
        pltpu.VMEM((BLK, WB * BLK), F32),
        pltpu.VMEM((BLK, WB * BLK), BF16),
        pltpu.VMEM((BLK, WB * BLK), BF16),
        pltpu.VMEM((NZ - 1, ROWS, WB * BLK), BF16),
        pltpu.VMEM((NZ - 1, ROWS, WB * BLK), BF16),
        pltpu.VMEM((HALF, BLK, BLK), BF16),
        pltpu.VMEM((HALF, BLK, BLK), BF16),
        dma((2,)),
        dma((2,)),
        dma((2, NZ - 1)),
        dma((2, NZ - 1)),
        dma((2, CHUNKS, 3)),
        dma((2, CHUNKS, 3)),
        dma((2, CHUNKS, 3)),
        dma((2, CHUNKS, 3)),
        dma((2, CHUNKS, 3)),
        dma((2, CHUNKS, 3)),
        dma((2, CHUNKS, 3)),
        dma((2, CHUNKS, 3)),
        dma((3, CHUNKS)),
        dma((3, CHUNKS)),
        dma((2, NZ - 1)),
        dma((2, NZ - 1)),
        dma((2, 3)),
    ]
    return pl.pallas_call(
        kernel,
        out_shape=(
            jax.ShapeDtypeStruct((ROWS, WB * BLK), BF16),
            jax.ShapeDtypeStruct((ROWS, WB * BLK), BF16),
            jax.ShapeDtypeStruct((1, 1, HALF, BLK, BLK), BF16),
            jax.ShapeDtypeStruct((1, 1, HALF, BLK, BLK), BF16),
        ),
        in_specs=[smem, smem, smem, anym, anym, anym, anym],
        out_specs=(vmem, vmem, anym, anym),
        scratch_shapes=scratch,
        compiler_params=pltpu.CompilerParams(
            collective_id=0, has_side_effects=True, vmem_limit_bytes=52 * 1024 * 1024
        ),
    )(inv, slots, counts, inputs, grad_out, up_blocks, down_blocks)


def solution(mesh):
    return jax.shard_map(
        on_device,
        mesh=mesh,
        in_specs=(
            P(("depth", "col"), "row"),
            P("row", "col", None, None, None),
            P("row", "col", None, None, None),
            P("row", "col", None),
            P("row", "col"),
            P(("depth", "col"), "row"),
        ),
        out_specs=(
            P(("depth", "col"), "row"),
            P(("depth", "col"), "row"),
            P("row", "col", "depth", None, None),
            P("row", "col", "depth", None, None),
        ),
        check_vma=False,
    )
```

```python
import jax
import jax.numpy as jnp
from jax import lax
from jax.experimental import pallas as pl
from jax.experimental.pallas import tpu as pltpu
from jax.sharding import PartitionSpec as P

MESH = pl.DeviceIdType.MESH
F32, BF16 = jnp.float32, jnp.bfloat16
BLK, CAP, HALF = 128, 108, 54
WB, FB = 6, 48
NX, NY, NZ = 4, 4, 8
CHUNKS = 3
ROWS = 16

root_coeff = 0.7978845608
cube_coeff = 0.044715


def gelu_parts(preact):
    cubed = preact * preact * preact
    tangent = jnp.tanh(root_coeff * (preact + cube_coeff * cubed))
    values = 0.5 * preact * (1.0 + tangent)
    slopes = 0.5 * (1.0 + tangent) + 0.5 * preact * (1.0 - tangent * tangent) * root_coeff * (
        1.0 + 3.0 * cube_coeff * preact * preact
    )
    return (values, slopes)


def dot(a, b):
    return lax.dot_general(a, b, (((1,), (0,)), ((), ())), preferred_element_type=F32)


def dot_t(a, b):
    return lax.dot_general(a, b, (((1,), (1,)), ((), ())), preferred_element_type=F32)


def quad(a, b, c, d):
    return jnp.concatenate(
        [jnp.concatenate([a, b], axis=1), jnp.concatenate([c, d], axis=1)], axis=0
    )


def kernel(
    inv_in, slots_in, counts_in, x_in, g_in, up_in, dn_in,
    out_ref, gin_ref, gup_ref, gdn_ref,
    inv, slots, counts, up, dn, xs, gs, xt, gt, pbuf, gbuf, r1p, r1g, s2p, s2g, ownp, owng, r2p, r2g,
    hid, pre, acc_o, acc_i, send_o, send_i, recv_o, recv_i,
    wsem, lsem, ssem_a, rsem_a, ssem_1, rsem_1, ssem_2, rsem_2, ssem_h, rsem_h, ssem_q, rsem_q,
    ssem_d, rsem_d, ssem_z, rsem_z, tsem,
):
    d, r, c = lax.axis_index("depth"), lax.axis_index("row"), lax.axis_index("col")
    y, x = r // NX, r % NX
    sends = []

    def at_x(o):
        return (d, y * NX + (x + o) % NX, c)

    def at_y(o):
        return (d, ((y + o) % NY) * NX + x, c)

    def at_z(o):
        return (d, r, (c + o) % NZ)

    partner = (1 - d, r, c)

    def remote(src, dst, ssem, rsem, device):
        copy = pltpu.make_async_remote_copy(
            src_ref=src, dst_ref=dst, send_sem=ssem, recv_sem=rsem, device_id=device, device_id_type=MESH
        )
        copy.start()
        sends.append(copy)
        return copy

    load_up = pltpu.make_async_copy(up_in.at[0, 0], up.at[pl.ds(0, CAP)], wsem.at[0])
    load_dn = pltpu.make_async_copy(dn_in.at[0, 0], dn.at[pl.ds(0, CAP)], wsem.at[1])
    mine = pl.ds(pl.multiple_of(c * ROWS, ROWS), ROWS)
    load_x = pltpu.make_async_copy(x_in, xs.at[0, mine], lsem.at[0])
    load_g = pltpu.make_async_copy(g_in, gs.at[0, mine], lsem.at[1])
    tables = [
        pltpu.make_async_copy(source, held, tsem.at[n])
        for n, (source, held) in enumerate(((inv_in, inv), (slots_in, slots), (counts_in, counts)))
    ]
    for copy in tables:
        copy.start()
    load_x.start()
    load_g.start()
    load_up.start()
    load_dn.start()
    up[CAP] = jnp.zeros((BLK, BLK), BF16)
    dn[CAP] = jnp.zeros((BLK, BLK), BF16)

    barrier = pltpu.get_barrier_semaphore()
    peers = [at_x(o) for o in (1, 2, 3)] + [at_y(o) for o in (1, 2, 3)]
    peers += [at_z(o) for o in range(1, NZ)] + [partner]
    for peer in peers:
        pl.semaphore_signal(barrier, inc=1, device_id=peer, device_id_type=MESH)
    pl.semaphore_wait(barrier, len(peers))

    far_first = (4, 3, 5, 2, 6, 1, 7)
    got_x, got_g = [], []
    for n, (src, dst, got) in enumerate(((x_in, xs, got_x), (g_in, gs, got_g))):
        for o in far_first:
            got.append(remote(src, dst.at[0, mine], ssem_a.at[n, o - 1], rsem_a.at[n, o - 1], at_z(o)))

    def block(weights, i, f):
        return weights[inv[i * FB + f]]

    def pair_p(fa, fb):
        acc = None
        for kk in range(3):
            w = quad(block(up, 2 * kk, fa), block(up, 2 * kk, fb), block(up, 2 * kk + 1, fa), block(up, 2 * kk + 1, fb))
            term = dot(xs[0, :, 256 * kk : 256 * kk + 256], w)
            acc = term if acc is None else acc + term
        return acc

    def pair_g(fa, fb):
        acc = None
        for kk in range(3):
            w = quad(block(dn, 2 * kk, fa), block(dn, 2 * kk + 1, fa), block(dn, 2 * kk, fb), block(dn, 2 * kk + 1, fb))
            term = dot_t(gs[0, :, 256 * kk : 256 * kk + 256], w)
            acc = term if acc is None else acc + term
        return acc

    got_1p, got_1g, got_2p, got_2g = {}, {}, {}, {}

    def make_p(k):
        for o in (2, 1, 3, 0):
            xx = (x + o) % NX

            for m in range(2):
                fa = 16 * k + 8 * m + xx
                acc = pair_p(fa, fa + NX).astype(BF16)
                pbuf[k, xx * 4 + 2 * m] = acc[:, :BLK]
                pbuf[k, xx * 4 + 2 * m + 1] = acc[:, BLK:]
            if o:
                got_1p[k, o] = remote(
                    pbuf.at[k, pl.ds(xx * 4, 4)], r1p.at[k, o - 1], ssem_1.at[0, k, o - 1], rsem_1.at[0, k, o - 1], at_x(o)
                )

    def make_g(k):
        for o in (2, 1, 3, 0):
            yy = (y + o) % NY

            for m in range(2):
                fa = 16 * k + 4 * yy + 2 * m
                acc = pair_g(fa, fa + 1).astype(BF16)
                gbuf[k, yy * 4 + 2 * m] = acc[:, :BLK]
                gbuf[k, yy * 4 + 2 * m + 1] = acc[:, BLK:]
            if o:
                got_1g[k, o] = remote(
                    gbuf.at[k, pl.ds(yy * 4, 4)], r1g.at[k, o - 1], ssem_1.at[1, k, o - 1], rsem_1.at[1, k, o - 1], at_y(o)
                )

    def second(k, n, buf, base, here, r1, s2, own, r2, got_1, got_2, at):
        for o in (1, 2, 3):
            got_1[k, o].wait_recv()
        for o in (2, 1, 3, 0):
            p = (here + o) % 4
            total = buf[k, base * 4 + p].astype(F32)
            for j in range(3):
                total = total + r1[k, j, p].astype(F32)
            if o:
                s2[k, p] = total.astype(BF16)
                got_2[k, o] = remote(s2.at[k, p], r2.at[k, o - 1], ssem_2.at[n, k, o - 1], rsem_2.at[n, k, o - 1], at(o))
            else:
                own[k] = total

    def second_p(k):
        second(k, 0, pbuf, x, y, r1p, s2p, ownp, r2p, got_1p, got_2p, at_y)

    def second_g(k):
        second(k, 1, gbuf, y, x, r1g, s2g, owng, r2g, got_1g, got_2g, at_x)

    got_h1, got_h2, got_q1, got_q2, got_d = {}, {}, {}, {}, {}
    hpos, qpos = x * 4 + y, y * 4 + x

    def activate(k):
        for o in (1, 2, 3):
            got_2p[k, o].wait_recv()
        p = ownp[k]
        for j in range(3):
            p = p + r2p[k, j].astype(F32)
        values, slopes = gelu_parts(p)
        hid[0, k, hpos] = values.astype(BF16)
        for o in (2, 1, 3):
            spot = hid.at[0, k, hpos]
            got_h1[k, o] = remote(spot, spot, ssem_h.at[0, k, o - 1], rsem_h.at[0, k, o - 1], at_y(o))
        for o in (1, 2, 3):
            got_2g[k, o].wait_recv()
        g = owng[k]
        for j in range(3):
            g = g + r2g[k, j].astype(F32)
        pre[0, k, qpos] = (g * slopes).astype(BF16)
        for o in (2, 1, 3):
            spot = pre.at[0, k, qpos]
            got_q1[k, o] = remote(spot, spot, ssem_q.at[0, k, o - 1], rsem_q.at[0, k, o - 1], at_x(o))

    def spread(k):
        for o in (1, 2, 3):
            got_h1[k, o].wait_recv()
        for o in (2, 1, 3):
            spot = hid.at[0, k, pl.ds(x * 4, 4)]
            got_h2[k, o] = remote(spot, spot, ssem_h.at[1, k, o - 1], rsem_h.at[1, k, o - 1], at_x(o))
        for o in (1, 2, 3):
            got_q1[k, o].wait_recv()
        for o in (2, 1, 3):
            spot = pre.at[0, k, pl.ds(y * 4, 4)]
            got_q2[k, o] = remote(spot, spot, ssem_q.at[1, k, o - 1], rsem_q.at[1, k, o - 1], at_y(o))

    def use_h(k):
        for o in (1, 2, 3):
            got_h2[k, o].wait_recv()
        got_d[0, k] = remote(hid.at[0, k], hid.at[1, k], ssem_d.at[0, k], rsem_d.at[0, k], partner)
        places = [(xx, yy) for xx in range(NX) for yy in range(NY)]
        h = jnp.concatenate([hid[0, k, xx * 4 + yy] for xx, yy in places], axis=1)
        for n in range(3):
            cols = slice(256 * n, 256 * n + 256)
            w = jnp.concatenate(
                [
                    jnp.concatenate([block(dn, 2 * n + u, 16 * k + 4 * yy + xx) for u in range(2)], axis=1)
                    for xx, yy in places
                ],
                axis=0,
            )
            part = dot(h, w)
            acc_o[:, cols] = part if k == 0 else acc_o[:, cols] + part

    def use_q(k):
        for o in (1, 2, 3):
            got_q2[k, o].wait_recv()
        got_d[1, k] = remote(pre.at[0, k], pre.at[1, k], ssem_d.at[1, k], rsem_d.at[1, k], partner)
        q = jnp.concatenate([pre[0, k, p] for p in range(16)], axis=1)
        for n in range(3):
            cols = slice(256 * n, 256 * n + 256)
            w = jnp.concatenate(
                [jnp.concatenate([block(up, 2 * n + u, 16 * k + p) for p in range(16)], axis=1) for u in range(2)],
                axis=0,
            )
            part = dot_t(q, w)
            acc_i[:, cols] = part if k == 0 else acc_i[:, cols] + part

    def scatter(n, acc, buf, recv):
        got = []
        buf[...] = acc[...].astype(BF16)
        for o in far_first:
            cc = (c + o) % NZ
            rows = pl.ds(pl.multiple_of(cc * ROWS, ROWS), ROWS)
            got.append(remote(buf.at[rows], recv.at[o - 1], ssem_z.at[n, o - 1], rsem_z.at[n, o - 1], at_z(o)))
        return got

    def gather_up(got, acc, recv, result):
        for copy in got:
            copy.wait_recv()
        total = acc[mine, :]
        for j in range(NZ - 1):
            total = total + recv[j].astype(F32)
        result[...] = total.astype(BF16)

    load_x.wait()
    for copy in got_x:
        copy.wait_recv()
    load_up.wait()
    for copy in tables:
        copy.wait()
    for k in range(CHUNKS):
        make_p(k)
    load_g.wait()
    for copy in got_g:
        copy.wait_recv()
    load_dn.wait()
    for k in range(CHUNKS):
        make_g(k)
    got_d["x"] = remote(xs.at[0], xs.at[1], ssem_d.at[2, 0], rsem_d.at[2, 0], partner)
    got_d["g"] = remote(gs.at[0], gs.at[1], ssem_d.at[2, 1], rsem_d.at[2, 1], partner)
    second_p(0)
    second_g(0)
    second_p(1)
    second_g(1)
    activate(0)
    second_p(2)
    second_g(2)
    activate(1)
    spread(0)
    activate(2)
    spread(1)
    got_d["x"].wait_recv()
    got_d["g"].wait_recv()
    for i in range(WB):
        cols = slice(BLK * i, BLK * i + BLK)
        for half in range(2):
            xt[i, :, BLK * half : BLK * half + BLK] = xs[half, :, cols].T
            gt[i, half] = gs[half, :, cols]
    spread(2)
    use_h(0)
    use_q(0)
    use_h(1)
    use_q(1)
    use_h(2)
    got_o = scatter(0, acc_o, send_o, recv_o)
    use_q(2)
    got_i = scatter(1, acc_i, send_i, recv_i)

    alive = counts[0, 0]

    def grad_down(s, carry):
        slot = d * HALF + s
        number = slots[0, 0, slot]
        i, f = number // FB, number % FB
        k, yy, xx = f // 16, (f % 16) // 4, f % 4
        hpair = jnp.concatenate([hid[0, k, xx * 4 + yy], hid[1, k, xx * 4 + yy]], axis=0)
        gpair = jnp.concatenate([gt[i, 0], gt[i, 1]], axis=0)
        part = lax.dot_general(hpair, gpair, (((0,), (0,)), ((), ())), preferred_element_type=F32)
        live = jnp.where(slot < alive, 1.0, 0.0)
        gdn_ref[0, 0, s] = (part * live).astype(BF16)
        return carry

    def grad_up(s, carry):
        slot = d * HALF + s
        number = slots[0, 0, slot]
        i, f = number // FB, number % FB
        k, yy, xx = f // 16, (f % 16) // 4, f % 4
        qpair = jnp.concatenate([pre[0, k, yy * 4 + xx], pre[1, k, yy * 4 + xx]], axis=0)
        part = dot(xt[i], qpair)
        live = jnp.where(slot < alive, 1.0, 0.0)
        gup_ref[0, 0, s] = (part * live).astype(BF16)
        return carry

    for k in range(CHUNKS):
        got_d[0, k].wait_recv()
    for part in range(3):
        lax.fori_loop(18 * part, 18 * part + 18, grad_down, 0, unroll=18)
    gather_up(got_o, acc_o, recv_o, out_ref)
    for k in range(CHUNKS):
        got_d[1, k].wait_recv()
    for part in range(3):
        lax.fori_loop(18 * part, 18 * part + 18, grad_up, 0, unroll=18)
    gather_up(got_i, acc_i, recv_i, gin_ref)
    for copy in sends:
        copy.wait_send()


def write_out(*refs):
    copies = [pltpu.make_async_copy(refs[n], refs[n + 4], refs[8].at[n]) for n in range(4)]
    for copy in copies:
        copy.start()
    for copy in copies:
        copy.wait()


def on_device(inputs, up_blocks, down_blocks, slots, counts, grad_out):
    places = jnp.arange(WB * FB, dtype=jnp.int32)
    order = jnp.arange(CAP, dtype=jnp.int32)
    held = (slots[0, 0][None, :] == places[:, None]) & (order < counts[0, 0])[None, :]
    inv = jnp.min(jnp.where(held, order[None, :], CAP), axis=1)
    vmem = pl.BlockSpec(memory_space=pltpu.VMEM)
    hbm = pl.BlockSpec(memory_space=pltpu.HBM)
    dma = pltpu.SemaphoreType.DMA
    scratch = [
        pltpu.SMEM((WB * FB,), jnp.int32),
        pltpu.SMEM((1, 1, CAP), jnp.int32),
        pltpu.SMEM((1, 1), jnp.int32),
        pltpu.VMEM((CAP + 1, BLK, BLK), BF16),
        pltpu.VMEM((CAP + 1, BLK, BLK), BF16),
        pltpu.VMEM((2, BLK, WB * BLK), BF16),
        pltpu.VMEM((2, BLK, WB * BLK), BF16),
        pltpu.VMEM((WB, BLK, 2 * BLK), BF16),
        pltpu.VMEM((WB, 2, BLK, BLK), BF16),
        pltpu.VMEM((CHUNKS, 16, BLK, BLK), BF16),
        pltpu.VMEM((CHUNKS, 16, BLK, BLK), BF16),
        pltpu.VMEM((CHUNKS, 3, 4, BLK, BLK), BF16),
        pltpu.VMEM((CHUNKS, 3, 4, BLK, BLK), BF16),
        pltpu.VMEM((CHUNKS, 4, BLK, BLK), BF16),
        pltpu.VMEM((CHUNKS, 4, BLK, BLK), BF16),
        pltpu.VMEM((CHUNKS, BLK, BLK), F32),
        pltpu.VMEM((CHUNKS, BLK, BLK), F32),
        pltpu.VMEM((CHUNKS, 3, BLK, BLK), BF16),
        pltpu.VMEM((CHUNKS, 3, BLK, BLK), BF16),
        pltpu.VMEM((2, CHUNKS, 16, BLK, BLK), BF16),
        pltpu.VMEM((2, CHUNKS, 16, BLK, BLK), BF16),
        pltpu.VMEM((BLK, WB * BLK), F32),
        pltpu.VMEM((BLK, WB * BLK), F32),
        pltpu.VMEM((BLK, WB * BLK), BF16),
        pltpu.VMEM((BLK, WB * BLK), BF16),
        pltpu.VMEM((NZ - 1, ROWS, WB * BLK), BF16),
        pltpu.VMEM((NZ - 1, ROWS, WB * BLK), BF16),
        dma((2,)),
        dma((2,)),
        dma((2, NZ - 1)),
        dma((2, NZ - 1)),
        dma((2, CHUNKS, 3)),
        dma((2, CHUNKS, 3)),
        dma((2, CHUNKS, 3)),
        dma((2, CHUNKS, 3)),
        dma((2, CHUNKS, 3)),
        dma((2, CHUNKS, 3)),
        dma((2, CHUNKS, 3)),
        dma((2, CHUNKS, 3)),
        dma((3, CHUNKS)),
        dma((3, CHUNKS)),
        dma((2, NZ - 1)),
        dma((2, NZ - 1)),
        dma((3,)),
    ]
    shapes = (
        jax.ShapeDtypeStruct((ROWS, WB * BLK), BF16),
        jax.ShapeDtypeStruct((ROWS, WB * BLK), BF16),
        jax.ShapeDtypeStruct((1, 1, HALF, BLK, BLK), BF16),
        jax.ShapeDtypeStruct((1, 1, HALF, BLK, BLK), BF16),
    )
    results = pl.pallas_call(
        kernel,
        out_shape=shapes,
        in_specs=[hbm] * 7,
        out_specs=(vmem,) * 4,
        scratch_shapes=scratch,
        compiler_params=pltpu.CompilerParams(
            collective_id=0, has_side_effects=True, vmem_limit_bytes=48 * 1024 * 1024
        ),
    )(inv, slots, counts, inputs, grad_out, up_blocks, down_blocks)
    return pl.pallas_call(
        write_out, out_shape=shapes, in_specs=[vmem] * 4, out_specs=(hbm,) * 4, scratch_shapes=[dma((4,))]
    )(*results)


def solution(mesh):
    return jax.shard_map(
        on_device,
        mesh=mesh,
        in_specs=(
            P(("depth", "col"), "row"),
            P("row", "col", None, None, None),
            P("row", "col", None, None, None),
            P("row", "col", None),
            P("row", "col"),
            P(("depth", "col"), "row"),
        ),
        out_specs=(
            P(("depth", "col"), "row"),
            P(("depth", "col"), "row"),
            P("row", "col", "depth", None, None),
            P("row", "col", "depth", None, None),
        ),
        check_vma=False,
    )
```

```python
import jax
import jax.numpy as jnp
from jax import lax
from jax.experimental import pallas as pl
from jax.experimental.pallas import tpu as pltpu
from jax.sharding import PartitionSpec as P

MESH = pl.DeviceIdType.MESH
F32, BF16 = jnp.float32, jnp.bfloat16
BLK, CAP, HALF = 128, 108, 54
WB, FB = 6, 48
NX, NY, NZ = 4, 4, 8
CHUNKS = 3
ROWS = 16
ORDER = (
    "w00m00m01m02w10m10m11f00f01m12f02f10f11s00s01s02f12x00x10s10",
    "s11a00a01s12a02t00a10d00d01a11a12d02d10r00r01d11d12r02r10u00",
    "r11u01r12u02z00u10u11u12z10g00c00g10c10",
)
ORDER = [part[i : i + 3] for part in ORDER for i in range(0, len(part), 3)]

root_coeff = 0.7978845608
cube_coeff = 0.044715


def gelu_parts(preact):
    cubed = preact * preact * preact
    tangent = jnp.tanh(root_coeff * (preact + cube_coeff * cubed))
    values = 0.5 * preact * (1.0 + tangent)
    slopes = 0.5 * (1.0 + tangent) + 0.5 * preact * (1.0 - tangent * tangent) * root_coeff * (
        1.0 + 3.0 * cube_coeff * preact * preact
    )
    return (values, slopes)


def dot(a, b):
    return lax.dot_general(a, b, (((1,), (0,)), ((), ())), preferred_element_type=F32)


def dot_t(a, b):
    return lax.dot_general(a, b, (((1,), (1,)), ((), ())), preferred_element_type=F32)


def quad(a, b, c, d):
    return jnp.concatenate(
        [jnp.concatenate([a, b], axis=1), jnp.concatenate([c, d], axis=1)], axis=0
    )


def kernel(
    inv_in, slots_in, counts_in, x_in, g_in, up_in, dn_in,
    out_ref, gin_ref, gup_ref, gdn_ref,
    inv, slots, counts, up, dn, xs, gs, xt, gt, farp, farg, nearp, nearg, keptp, keptg, thrup, thrug, joinp, joing, r1p, r1g, s2p, s2g, ownp, owng, slopes, r2p, r2g,
    hid, pre, acc_o, acc_i, send_o, send_i, recv_o, recv_i,
    wsem, lsem, ssem_a, rsem_a, ssem_1, rsem_1, ssem_2, rsem_2, ssem_h, rsem_h, ssem_q, rsem_q, ssem_h4, rsem_h4, ssem_q4, rsem_q4,
    ssem_d, rsem_d, ssem_z, rsem_z, tsem,
):
    d, r, c = lax.axis_index("depth"), lax.axis_index("row"), lax.axis_index("col")
    y, x = r // NX, r % NX
    sends = []

    def at_x(o):
        return (d, y * NX + (x + o) % NX, c)

    def at_y(o):
        return (d, ((y + o) % NY) * NX + x, c)

    def at_z(o):
        return (d, r, (c + o) % NZ)

    partner = (1 - d, r, c)

    def remote(src, dst, ssem, rsem, device):
        copy = pltpu.make_async_remote_copy(
            src_ref=src, dst_ref=dst, send_sem=ssem, recv_sem=rsem, device_id=device, device_id_type=MESH
        )
        copy.start()
        sends.append(copy)
        return copy

    load_up = pltpu.make_async_copy(up_in.at[0, 0], up.at[pl.ds(0, CAP)], wsem.at[0])
    load_dn = pltpu.make_async_copy(dn_in.at[0, 0], dn.at[pl.ds(0, CAP)], wsem.at[1])
    mine = pl.ds(pl.multiple_of(c * ROWS, ROWS), ROWS)
    load_x = pltpu.make_async_copy(x_in, xs.at[0, mine], lsem.at[0])
    load_g = pltpu.make_async_copy(g_in, gs.at[0, mine], lsem.at[1])
    tables = [
        pltpu.make_async_copy(source, held, tsem.at[n])
        for n, (source, held) in enumerate(((inv_in, inv), (slots_in, slots), (counts_in, counts)))
    ]
    for copy in tables:
        copy.start()
    load_x.start()
    load_g.start()
    load_up.start()
    load_dn.start()
    up[CAP] = jnp.zeros((BLK, BLK), BF16)
    dn[CAP] = jnp.zeros((BLK, BLK), BF16)

    barrier = pltpu.get_barrier_semaphore()
    peers = [at_x(o) for o in (1, 2, 3)] + [at_y(o) for o in (1, 2, 3)]
    peers += [at_z(o) for o in range(1, NZ)] + [partner]
    for peer in peers:
        pl.semaphore_signal(barrier, inc=1, device_id=peer, device_id_type=MESH)
    pl.semaphore_wait(barrier, len(peers))

    got_x, got_g = [], []
    for n, (load, held, got) in enumerate(((load_x, xs, got_x), (load_g, gs, got_g))):
        load.wait()
        spot = held.at[0, mine]
        for o in (4, 3, 5, 2, 6, 1, 7):
            got.append(remote(spot, spot, ssem_a.at[n, o], rsem_a.at[n, o], at_z(o)))

    def block(weights, i, f):
        return weights[inv[i * FB + f]]

    def pair_p(fa, fb):
        acc = None
        for kk in range(3):
            w = quad(block(up, 2 * kk, fa), block(up, 2 * kk, fb), block(up, 2 * kk + 1, fa), block(up, 2 * kk + 1, fb))
            term = dot(xs[0, :, 256 * kk : 256 * kk + 256], w)
            acc = term if acc is None else acc + term
        return acc

    def pair_g(fa, fb):
        acc = None
        for kk in range(3):
            w = quad(block(dn, 2 * kk, fa), block(dn, 2 * kk + 1, fa), block(dn, 2 * kk, fb), block(dn, 2 * kk + 1, fb))
            term = dot_t(gs[0, :, 256 * kk : 256 * kk + 256], w)
            acc = term if acc is None else acc + term
        return acc

    far, near_out, kept, through, joined = (farp, farg), (nearp, nearg), (keptp, keptg), (thrup, thrug), (joinp, joing)
    first_in, second_out, own, second_in = (r1p, r1g), (s2p, s2g), (ownp, owng), (r2p, r2g)
    gathered, gsem, gsem4 = (hid, pre), ((ssem_h, rsem_h), (ssem_q, rsem_q)), ((ssem_h4, rsem_h4), (ssem_q4, rsem_q4))
    got_1, got_2, got_3, got_4, got_d = {}, {}, {}, {}, {}

    def x_first(n, k):
        return (n + k) % 2 == 0

    def axes(n, k):
        return (x, at_x, y, at_y) if x_first(n, k) else (y, at_y, x, at_x)

    def hidden_block(n, k, a, b):
        return 16 * k + (4 * b + a if x_first(n, k) else 4 * a + b)

    def send_1(n, k, i, src, dst, at):
        got_1[n, k, i] = remote(src, dst, ssem_1.at[n, k, i], rsem_1.at[n, k, i], at(3 if i % 2 else 1))

    def make(n, k):
        here, at, _, _ = axes(n, k)

        def product(o, m):
            a = (here + o) % 4
            return (pair_p, pair_g)[n](hidden_block(n, k, a, 2 * m), hidden_block(n, k, a, 2 * m + 1))

        def keep(ref, where, value):
            ref[where] = value[:, :BLK].astype(ref.dtype)
            ref[(*where[:-1], where[-1] + 1)] = value[:, BLK:].astype(ref.dtype)

        for m in range(2):
            keep(far[n], (k, 2 * m), product(2, m))
            send_1(n, k, m, far[n].at[k, pl.ds(2 * m, 2)], through[n].at[k, m], at)
        for way, o in ((0, 1), (1, 3)):
            keep(near_out[n], (k, way, 0), product(o, 1 - way))
            send_1(n, k, 2 + way, near_out[n].at[k, way, pl.ds(0, 2)], first_in[n].at[k, 1 + way, pl.ds(2 - 2 * way, 2)], at)
        for way, o in ((0, 1), (1, 3)):
            keep(kept[n], (k, 4 + 2 * way), product(o, way))
        for m in range(2):
            keep(kept[n], (k, 2 * m), product(0, m))

    def forward(n, k):
        _, at, _, _ = axes(n, k)
        for way in range(2):
            got_1[n, k, way].wait_recv()
            for i in range(2):
                total = kept[n][k, 4 + 2 * way + i] + through[n][k, way, i].astype(F32)
                joined[n][k, way, i] = total.astype(BF16)
            send_1(n, k, 4 + way, joined[n].at[k, way], first_in[n].at[k, 1 + way, pl.ds(2 * way, 2)], at)

    def second(n, k):
        _, _, here, at = axes(n, k)
        for i in range(2, 6):
            got_1[n, k, i].wait_recv()
        for o in (2, 1, 3, 0):
            b = (here + o) % 4
            total = kept[n][k, b]
            for i in range(1, 3):
                total = total + first_in[n][k, i, b].astype(F32)
            if o:
                second_out[n][k, b] = total.astype(BF16)
                got_2[n, k, o] = remote(
                    second_out[n].at[k, b], second_in[n].at[k, o - 1], ssem_2.at[n, k, o - 1], rsem_2.at[n, k, o - 1], at(o)
                )
            else:
                own[n][k] = total

    def summed(n, k):
        for o in (1, 2, 3):
            got_2[n, k, o].wait_recv()
        total = own[n][k]
        for j in range(3):
            total = total + second_in[n][k, j].astype(F32)
        return total

    def hand_out(n, k, share):
        a, _, b, at = axes(n, k)
        spot = gathered[n].at[0, k, a * 4 + b]
        gathered[n][0, k, a * 4 + b] = share.astype(BF16)
        for o in (2, 1, 3):
            got_3[n, k, o] = remote(spot, spot, gsem[n][0].at[k, o - 1], gsem[n][1].at[k, o - 1], at(o))

    def activate_h(k):
        values, slope = gelu_parts(summed(0, k))
        slopes[k] = slope
        hand_out(0, k, values)

    def activate_q(k):
        hand_out(1, k, summed(1, k) * slopes[k])

    def send_4(n, k, i, first, at):
        spot = gathered[n].at[0, k, pl.ds(first, 2)]
        got_4[n, k, i] = remote(spot, spot, gsem4[n][0].at[k, i], gsem4[n][1].at[k, i], at(3 if i % 2 else 1))

    def spread(n, k):
        a, at, _, _ = axes(n, k)
        for o in (1, 2, 3):
            got_3[n, k, o].wait_recv()
        for i, first in enumerate((0, 2, 2, 0)):
            send_4(n, k, i, a * 4 + first, at)

    def relay(n, k):
        a, at, _, _ = axes(n, k)
        for way, o in ((0, 3), (1, 1)):
            got_4[n, k, way].wait_recv()
            send_4(n, k, 4 + way, (a + o) % 4 * 4 + 2 * way, at)

    def use(n, k):
        for i in range(2, 6):
            got_4[n, k, i].wait_recv()
        got_d[n, k] = remote(gathered[n].at[0, k], gathered[n].at[1, k], ssem_d.at[n, k], rsem_d.at[n, k], partner)
        weights, acc = ((dn, acc_o), (up, acc_i))[n]
        blocks = [hidden_block(n, k, p // 4, p % 4) for p in range(16)]
        left = jnp.concatenate([gathered[n][0, k, p] for p in range(16)], axis=1)
        for m in range(3):
            cols = slice(256 * m, 256 * m + 256)
            if n == 0:
                w = [jnp.concatenate([block(weights, 2 * m + u, f) for u in range(2)], axis=1) for f in blocks]
                part = dot(left, jnp.concatenate(w, axis=0))
            else:
                w = [jnp.concatenate([block(weights, 2 * m + u, f) for f in blocks], axis=1) for u in range(2)]
                part = dot_t(left, jnp.concatenate(w, axis=0))
            acc[:, cols] = part if k == 0 else acc[:, cols] + part

    def scatter(n, acc, buf, recv):
        got = []
        buf[...] = acc[...].astype(BF16)
        for o in (4, 3, 5, 2, 6, 1, 7):
            cc = (c + o) % NZ
            rows = pl.ds(pl.multiple_of(cc * ROWS, ROWS), ROWS)
            got.append(remote(buf.at[rows], recv.at[o - 1], ssem_z.at[n, o - 1], rsem_z.at[n, o - 1], at_z(o)))
        return got

    def gather_up(got, acc, recv, result):
        for copy in got:
            copy.wait_recv()
        total = acc[mine, :]
        for j in range(NZ - 1):
            total = total + recv[j].astype(F32)
        result[...] = total.astype(BF16)

    def grad_down(s, carry):
        slot = d * HALF + s
        number = slots[0, 0, slot]
        i, f = number // FB, number % FB
        k, yy, xx = f // 16, (f % 16) // 4, f % 4
        p = jnp.where(k == 1, yy * 4 + xx, xx * 4 + yy)
        hpair = jnp.concatenate([hid[0, k, p], hid[1, k, p]], axis=0)
        gpair = jnp.concatenate([gt[i, 0], gt[i, 1]], axis=0)
        part = lax.dot_general(hpair, gpair, (((0,), (0,)), ((), ())), preferred_element_type=F32)
        live = jnp.where(slot < counts[0, 0], 1.0, 0.0)
        gdn_ref[0, 0, s] = (part * live).astype(BF16)
        return carry

    def grad_up(s, carry):
        slot = d * HALF + s
        number = slots[0, 0, slot]
        i, f = number // FB, number % FB
        k, yy, xx = f // 16, (f % 16) // 4, f % 4
        p = jnp.where(k == 1, xx * 4 + yy, yy * 4 + xx)
        qpair = jnp.concatenate([pre[0, k, p], pre[1, k, p]], axis=0)
        part = dot(xt[i], qpair)
        live = jnp.where(slot < counts[0, 0], 1.0, 0.0)
        gup_ref[0, 0, s] = (part * live).astype(BF16)
        return carry

    def activate(n, k):
        (activate_h, activate_q)[n](k)

    def wait_tokens(n, k):
        for copy in (got_x, got_g)[n]:
            copy.wait_recv()
        (load_up, load_dn)[n].wait()
        if n == 0:
            for copy in tables:
                copy.wait()

    def swap_tokens(n, k):
        held = (xs, gs)[n]
        got_d["xg"[n]] = remote(held.at[0], held.at[1], ssem_d.at[2, n], rsem_d.at[2, n], partner)

    def turn(n, k):
        got_d["x"].wait_recv()
        got_d["g"].wait_recv()
        for i in range(WB):
            cols = slice(BLK * i, BLK * i + BLK)
            for half in range(2):
                xt[i, :, BLK * half : BLK * half + BLK] = xs[half, :, cols].T
                gt[i, half] = gs[half, :, cols]

    got_z = {}

    def scatter_out(n, k):
        got_z[n] = scatter(n, (acc_o, acc_i)[n], (send_o, send_i)[n], (recv_o, recv_i)[n])

    def collect(n, k):
        gather_up(got_z[n], (acc_o, acc_i)[n], (recv_o, recv_i)[n], (out_ref, gin_ref)[n])

    def gradients(n, k):
        for j in range(CHUNKS):
            got_d[n, j].wait_recv()
        for part in range(3):
            lax.fori_loop(18 * part, 18 * part + 18, (grad_down, grad_up)[n], 0, unroll=18)

    steps = dict(
        w=wait_tokens, x=swap_tokens, m=make, f=forward, s=second, a=activate, d=spread, r=relay, u=use, t=turn, z=scatter_out, c=collect, g=gradients
    )
    for step in ORDER:
        steps[step[0]](int(step[1]), int(step[2]))
    for copy in sends:
        copy.wait_send()


def write_out(*refs):
    copies = [pltpu.make_async_copy(refs[n], refs[n + 4], refs[8].at[n]) for n in range(4)]
    for copy in copies:
        copy.start()
    for copy in copies:
        copy.wait()


def on_device(inputs, up_blocks, down_blocks, slots, counts, grad_out):
    places = jnp.arange(WB * FB, dtype=jnp.int32)
    order = jnp.arange(CAP, dtype=jnp.int32)
    match = (slots[0, 0][None, :] == places[:, None]) & (order < counts[0, 0])[None, :]
    inv = jnp.min(jnp.where(match, order[None, :], CAP), axis=1)
    vmem = pl.BlockSpec(memory_space=pltpu.VMEM)
    anym = pl.BlockSpec(memory_space=pl.ANY)
    hbm = pl.BlockSpec(memory_space=pltpu.HBM)
    dma = pltpu.SemaphoreType.DMA
    scratch = [
        pltpu.SMEM((WB * FB,), jnp.int32),
        pltpu.SMEM((1, 1, CAP), jnp.int32),
        pltpu.SMEM((1, 1), jnp.int32),
        pltpu.VMEM((CAP + 1, BLK, BLK), BF16),
        pltpu.VMEM((CAP + 1, BLK, BLK), BF16),
        pltpu.VMEM((2, BLK, WB * BLK), BF16),
        pltpu.VMEM((2, BLK, WB * BLK), BF16),
        pltpu.VMEM((WB, BLK, 2 * BLK), BF16),
        pltpu.VMEM((WB, 2, BLK, BLK), BF16),
        pltpu.VMEM((CHUNKS, 4, BLK, BLK), BF16),
        pltpu.VMEM((CHUNKS, 4, BLK, BLK), BF16),
        pltpu.VMEM((CHUNKS, 2, 4, BLK, BLK), BF16),
        pltpu.VMEM((CHUNKS, 2, 4, BLK, BLK), BF16),
        pltpu.VMEM((CHUNKS, 8, BLK, BLK), F32),
        pltpu.VMEM((CHUNKS, 8, BLK, BLK), F32),
        pltpu.VMEM((CHUNKS, 2, 2, BLK, BLK), BF16),
        pltpu.VMEM((CHUNKS, 2, 2, BLK, BLK), BF16),
        pltpu.VMEM((CHUNKS, 2, 2, BLK, BLK), BF16),
        pltpu.VMEM((CHUNKS, 2, 2, BLK, BLK), BF16),
        pltpu.VMEM((CHUNKS, 3, 4, BLK, BLK), BF16),
        pltpu.VMEM((CHUNKS, 3, 4, BLK, BLK), BF16),
        pltpu.VMEM((CHUNKS, 4, BLK, BLK), BF16),
        pltpu.VMEM((CHUNKS, 4, BLK, BLK), BF16),
        pltpu.VMEM((CHUNKS, BLK, BLK), F32),
        pltpu.VMEM((CHUNKS, BLK, BLK), F32),
        pltpu.VMEM((CHUNKS, BLK, BLK), F32),
        pltpu.VMEM((CHUNKS, 3, BLK, BLK), BF16),
        pltpu.VMEM((CHUNKS, 3, BLK, BLK), BF16),
        pltpu.VMEM((2, CHUNKS, 16, BLK, BLK), BF16),
        pltpu.VMEM((2, CHUNKS, 16, BLK, BLK), BF16),
        pltpu.VMEM((BLK, WB * BLK), F32),
        pltpu.VMEM((BLK, WB * BLK), F32),
        pltpu.VMEM((BLK, WB * BLK), BF16),
        pltpu.VMEM((BLK, WB * BLK), BF16),
        pltpu.VMEM((NZ - 1, ROWS, WB * BLK), BF16),
        pltpu.VMEM((NZ - 1, ROWS, WB * BLK), BF16),
        dma((2,)),
        dma((2,)),
        dma((2, NZ)),
        dma((2, NZ)),
        dma((2, CHUNKS, 6)),
        dma((2, CHUNKS, 6)),
        dma((2, CHUNKS, 3)),
        dma((2, CHUNKS, 3)),
        dma((CHUNKS, 3)),
        dma((CHUNKS, 3)),
        dma((CHUNKS, 3)),
        dma((CHUNKS, 3)),
        dma((CHUNKS, 6)),
        dma((CHUNKS, 6)),
        dma((CHUNKS, 6)),
        dma((CHUNKS, 6)),
        dma((3, CHUNKS)),
        dma((3, CHUNKS)),
        dma((2, NZ - 1)),
        dma((2, NZ - 1)),
        dma((3,)),
    ]
    held = [pltpu.with_memory_space_constraint(a, pltpu.HBM) for a in (slots, inputs, grad_out, up_blocks, down_blocks)]
    shapes = (
        jax.ShapeDtypeStruct((ROWS, WB * BLK), BF16),
        jax.ShapeDtypeStruct((ROWS, WB * BLK), BF16),
        jax.ShapeDtypeStruct((1, 1, HALF, BLK, BLK), BF16),
        jax.ShapeDtypeStruct((1, 1, HALF, BLK, BLK), BF16),
    )
    results = pl.pallas_call(
        kernel,
        out_shape=shapes,
        in_specs=[hbm] * 7,
        out_specs=(vmem,) * 4,
        scratch_shapes=scratch,
        compiler_params=pltpu.CompilerParams(
            collective_id=0, has_side_effects=True, vmem_limit_bytes=48 * 1024 * 1024
        ),
    )(inv, held[0], counts, *held[1:])
    return pl.pallas_call(
        write_out, out_shape=shapes, in_specs=[anym] * 4, out_specs=(hbm,) * 4, scratch_shapes=[dma((4,))],
        compiler_params=pltpu.CompilerParams(vmem_limit_bytes=4 * 1024 * 1024),
    )(*results)


def solution(mesh):
    return jax.shard_map(
        on_device,
        mesh=mesh,
        in_specs=(
            P(("depth", "col"), "row"),
            P("row", "col", None, None, None),
            P("row", "col", None, None, None),
            P("row", "col", None),
            P("row", "col"),
            P(("depth", "col"), "row"),
        ),
        out_specs=(
            P(("depth", "col"), "row"),
            P(("depth", "col"), "row"),
            P("row", "col", "depth", None, None),
            P("row", "col", "depth", None, None),
        ),
        check_vma=False,
    )
```

```python
import jax
import jax.numpy as jnp
from jax import lax
from jax.experimental import pallas as pl
from jax.experimental.pallas import tpu as pltpu
from jax.sharding import PartitionSpec as P

MESH = pl.DeviceIdType.MESH
F32, BF16 = jnp.float32, jnp.bfloat16
BLK, CAP, HALF = 128, 108, 54
WB, FB = 6, 48
NX, NY, NZ = 4, 4, 8
CHUNKS = 3
ROWS = 16
ORDER = (
    "w00m00m01m02w10m10m11f00f01m12f02f10f11s00s01s02f12x00x10s10",
    "s11a00a01s12a02t00a10d00d01a11a12d02d10r00r01d11d12r02r10u00",
    "r11u01r12u02z00u10u11u12z10g00c00g10e00c10",
)
ORDER = [part[i : i + 3] for part in ORDER for i in range(0, len(part), 3)]

root_coeff = 0.7978845608
cube_coeff = 0.044715


def gelu_parts(preact):
    cubed = preact * preact * preact
    tangent = jnp.tanh(root_coeff * (preact + cube_coeff * cubed))
    values = 0.5 * preact * (1.0 + tangent)
    slopes = 0.5 * (1.0 + tangent) + 0.5 * preact * (1.0 - tangent * tangent) * root_coeff * (
        1.0 + 3.0 * cube_coeff * preact * preact
    )
    return (values, slopes)


def dot(a, b):
    return lax.dot_general(a, b, (((1,), (0,)), ((), ())), preferred_element_type=F32)


def dot_t(a, b):
    return lax.dot_general(a, b, (((1,), (1,)), ((), ())), preferred_element_type=F32)


def quad(a, b, c, d):
    return jnp.concatenate(
        [jnp.concatenate([a, b], axis=1), jnp.concatenate([c, d], axis=1)], axis=0
    )


def kernel(
    slots_in, counts, x_in, g_in, up_in, dn_in,
    out_ref, gin_ref, gup_ref, gdn_ref,
    inv, places, slots, up, dn, xs, gs, xt, gt, farp, farg, nearp, nearg, keptp, keptg, thrup, thrug, joinp, joing, r1p, r1g, s2p, s2g, ownp, owng, slopes, r2p, r2g,
    hid, pre, acc_o, acc_i, send_o, send_i, recv_o, recv_i,
    wsem, lsem, ssem_a, rsem_a, ssem_1, rsem_1, ssem_2, rsem_2, ssem_h, rsem_h, ssem_q, rsem_q, ssem_h4, rsem_h4, ssem_q4, rsem_q4,
    ssem_d, rsem_d, ssem_z, rsem_z, tsem,
):
    d, r, c = lax.axis_index("depth"), lax.axis_index("row"), lax.axis_index("col")
    y, x = r // NX, r % NX
    sends = []

    def at_x(o):
        return (d, y * NX + (x + o) % NX, c)

    def at_y(o):
        return (d, ((y + o) % NY) * NX + x, c)

    def at_z(o):
        return (d, r, (c + o) % NZ)

    partner = (1 - d, r, c)

    def remote(src, dst, ssem, rsem, device):
        copy = pltpu.make_async_remote_copy(
            src_ref=src, dst_ref=dst, send_sem=ssem, recv_sem=rsem, device_id=device, device_id_type=MESH
        )
        copy.start()
        sends.append(copy)
        return copy

    load_up = pltpu.make_async_copy(up_in.at[0, 0], up.at[pl.ds(0, CAP)], wsem.at[0])
    load_dn = pltpu.make_async_copy(dn_in.at[0, 0], dn.at[pl.ds(0, CAP)], wsem.at[1])
    mine = pl.ds(pl.multiple_of(c * ROWS, ROWS), ROWS)
    load_x = pltpu.make_async_copy(x_in, xs.at[0, mine], lsem.at[0])
    load_g = pltpu.make_async_copy(g_in, gs.at[0, mine], lsem.at[1])
    load_slots = pltpu.make_async_copy(slots_in, slots, tsem.at[0])
    load_slots.start()
    load_x.start()
    load_g.start()
    load_up.start()
    load_dn.start()
    up[CAP] = jnp.zeros((BLK, BLK), BF16)
    dn[CAP] = jnp.zeros((BLK, BLK), BF16)

    barrier = pltpu.get_barrier_semaphore()
    peers = [at_x(o) for o in (1, 2, 3)] + [at_y(o) for o in (1, 2, 3)]
    peers += [at_z(o) for o in range(1, NZ)] + [partner]
    for peer in peers:
        pl.semaphore_signal(barrier, inc=1, device_id=peer, device_id_type=MESH)
    pl.semaphore_wait(barrier, len(peers))

    got_x, got_g = [], []
    for n, (load, held, got) in enumerate(((load_x, xs, got_x), (load_g, gs, got_g))):
        load.wait()
        spot = held.at[0, mine]
        for o in (4, 3, 5, 2, 6, 1, 7):
            got.append(remote(spot, spot, ssem_a.at[n, o], rsem_a.at[n, o], at_z(o)))

    load_slots.wait()
    tile = (8, BLK)
    row, lane = lax.broadcasted_iota(jnp.int32, tile, 0), lax.broadcasted_iota(jnp.int32, tile, 1)
    number = jnp.where(lane < FB, row * FB + lane, WB * FB + BLK)

    def enter(slot, table):
        wanted = jnp.where(slot < counts[0, 0], slots[0, 0, slot], -1)
        return jnp.where(number == wanted, slot, table)

    places[...] = lax.fori_loop(0, CAP, enter, jnp.full(tile, CAP, jnp.int32), unroll=12)
    to_scalars = pltpu.make_async_copy(places, inv, tsem.at[1])
    to_scalars.start()

    def block(weights, i, f):
        return weights[inv[i, f]]

    def pair_p(fa, fb):
        acc = None
        for kk in range(3):
            w = quad(block(up, 2 * kk, fa), block(up, 2 * kk, fb), block(up, 2 * kk + 1, fa), block(up, 2 * kk + 1, fb))
            term = dot(xs[0, :, 256 * kk : 256 * kk + 256], w)
            acc = term if acc is None else acc + term
        return acc

    def pair_g(fa, fb):
        acc = None
        for kk in range(3):
            w = quad(block(dn, 2 * kk, fa), block(dn, 2 * kk + 1, fa), block(dn, 2 * kk, fb), block(dn, 2 * kk + 1, fb))
            term = dot_t(gs[0, :, 256 * kk : 256 * kk + 256], w)
            acc = term if acc is None else acc + term
        return acc

    far, near_out, kept, through, joined = (farp, farg), (nearp, nearg), (keptp, keptg), (thrup, thrug), (joinp, joing)
    first_in, second_out, own, second_in = (r1p, r1g), (s2p, s2g), (ownp, owng), (r2p, r2g)
    gathered, gsem, gsem4 = (hid, pre), ((ssem_h, rsem_h), (ssem_q, rsem_q)), ((ssem_h4, rsem_h4), (ssem_q4, rsem_q4))
    got_1, got_2, got_3, got_4, got_d = {}, {}, {}, {}, {}

    def x_first(n, k):
        return (n + k) % 2 == 0

    def axes(n, k):
        return (x, at_x, y, at_y) if x_first(n, k) else (y, at_y, x, at_x)

    def hidden_block(n, k, a, b):
        return 16 * k + (4 * b + a if x_first(n, k) else 4 * a + b)

    def send_1(n, k, i, src, dst, at):
        got_1[n, k, i] = remote(src, dst, ssem_1.at[n, k, i], rsem_1.at[n, k, i], at(3 if i % 2 else 1))

    def make(n, k):
        here, at, _, _ = axes(n, k)

        def product(o, m):
            a = (here + o) % 4
            return (pair_p, pair_g)[n](hidden_block(n, k, a, 2 * m), hidden_block(n, k, a, 2 * m + 1))

        def keep(ref, where, value):
            ref[where] = value[:, :BLK].astype(ref.dtype)
            ref[(*where[:-1], where[-1] + 1)] = value[:, BLK:].astype(ref.dtype)

        for m in range(2):
            keep(far[n], (k, 2 * m), product(2, m))
            send_1(n, k, m, far[n].at[k, pl.ds(2 * m, 2)], through[n].at[k, m], at)
        for way, o in ((0, 1), (1, 3)):
            keep(near_out[n], (k, way, 0), product(o, 1 - way))
            send_1(n, k, 2 + way, near_out[n].at[k, way, pl.ds(0, 2)], first_in[n].at[k, 1 + way, pl.ds(2 - 2 * way, 2)], at)
        for way, o in ((0, 1), (1, 3)):
            keep(kept[n], (k, 4 + 2 * way), product(o, way))
        for m in range(2):
            keep(kept[n], (k, 2 * m), product(0, m))

    def forward(n, k):
        _, at, _, _ = axes(n, k)
        for way in range(2):
            got_1[n, k, way].wait_recv()
            for i in range(2):
                total = kept[n][k, 4 + 2 * way + i] + through[n][k, way, i].astype(F32)
                joined[n][k, way, i] = total.astype(BF16)
            send_1(n, k, 4 + way, joined[n].at[k, way], first_in[n].at[k, 1 + way, pl.ds(2 * way, 2)], at)

    def second(n, k):
        _, _, here, at = axes(n, k)
        for i in range(2, 6):
            got_1[n, k, i].wait_recv()
        for o in (2, 1, 3, 0):
            b = (here + o) % 4
            total = kept[n][k, b]
            for i in range(1, 3):
                total = total + first_in[n][k, i, b].astype(F32)
            if o:
                second_out[n][k, b] = total.astype(BF16)
                got_2[n, k, o] = remote(
                    second_out[n].at[k, b], second_in[n].at[k, o - 1], ssem_2.at[n, k, o - 1], rsem_2.at[n, k, o - 1], at(o)
                )
            else:
                own[n][k] = total

    def summed(n, k):
        for o in (1, 2, 3):
            got_2[n, k, o].wait_recv()
        total = own[n][k]
        for j in range(3):
            total = total + second_in[n][k, j].astype(F32)
        return total

    def hand_out(n, k, share):
        a, _, b, at = axes(n, k)
        spot = gathered[n].at[0, k, a * 4 + b]
        gathered[n][0, k, a * 4 + b] = share.astype(BF16)
        for o in (2, 1, 3):
            got_3[n, k, o] = remote(spot, spot, gsem[n][0].at[k, o - 1], gsem[n][1].at[k, o - 1], at(o))

    def activate_h(k):
        values, slope = gelu_parts(summed(0, k))
        slopes[k] = slope
        hand_out(0, k, values)

    def activate_q(k):
        hand_out(1, k, summed(1, k) * slopes[k])

    def send_4(n, k, i, first, at):
        spot = gathered[n].at[0, k, pl.ds(first, 2)]
        got_4[n, k, i] = remote(spot, spot, gsem4[n][0].at[k, i], gsem4[n][1].at[k, i], at(3 if i % 2 else 1))

    def spread(n, k):
        a, at, _, _ = axes(n, k)
        for o in (1, 2, 3):
            got_3[n, k, o].wait_recv()
        for i, first in enumerate((0, 2, 2, 0)):
            send_4(n, k, i, a * 4 + first, at)

    def relay(n, k):
        a, at, _, _ = axes(n, k)
        for way, o in ((0, 3), (1, 1)):
            got_4[n, k, way].wait_recv()
            send_4(n, k, 4 + way, (a + o) % 4 * 4 + 2 * way, at)

    def use(n, k):
        for i in range(2, 6):
            got_4[n, k, i].wait_recv()
        got_d[n, k] = remote(gathered[n].at[0, k], gathered[n].at[1, k], ssem_d.at[n, k], rsem_d.at[n, k], partner)
        weights, acc = ((dn, acc_o), (up, acc_i))[n]
        blocks = [hidden_block(n, k, p // 4, p % 4) for p in range(16)]
        left = jnp.concatenate([gathered[n][0, k, p] for p in range(16)], axis=1)
        for m in range(3):
            cols = slice(256 * m, 256 * m + 256)
            if n == 0:
                w = [jnp.concatenate([block(weights, 2 * m + u, f) for u in range(2)], axis=1) for f in blocks]
                part = dot(left, jnp.concatenate(w, axis=0))
            else:
                w = [jnp.concatenate([block(weights, 2 * m + u, f) for f in blocks], axis=1) for u in range(2)]
                part = dot_t(left, jnp.concatenate(w, axis=0))
            acc[:, cols] = part if k == 0 else acc[:, cols] + part

    def scatter(n, acc, buf, recv):
        got = []
        buf[...] = acc[...].astype(BF16)
        for o in (4, 3, 5, 2, 6, 1, 7):
            cc = (c + o) % NZ
            rows = pl.ds(pl.multiple_of(cc * ROWS, ROWS), ROWS)
            got.append(remote(buf.at[rows], recv.at[o - 1], ssem_z.at[n, o - 1], rsem_z.at[n, o - 1], at_z(o)))
        return got

    def gather_up(got, acc, recv, result):
        for copy in got:
            copy.wait_recv()
        total = acc[mine, :]
        for j in range(NZ - 1):
            total = total + recv[j].astype(F32)
        result[...] = total.astype(BF16)

    def grad_down(s, carry):
        slot = d * HALF + s
        number = slots[0, 0, slot]
        i, f = number // FB, number % FB
        k, yy, xx = f // 16, (f % 16) // 4, f % 4
        p = jnp.where(k == 1, yy * 4 + xx, xx * 4 + yy)
        hpair = jnp.concatenate([hid[0, k, p], hid[1, k, p]], axis=0)
        gpair = jnp.concatenate([gt[i, 0], gt[i, 1]], axis=0)
        part = lax.dot_general(hpair, gpair, (((0,), (0,)), ((), ())), preferred_element_type=F32)
        live = jnp.where(slot < counts[0, 0], 1.0, 0.0)
        gdn_ref[0, 0, s] = (part * live).astype(BF16)
        return carry

    def grad_up(s, carry):
        slot = d * HALF + s
        number = slots[0, 0, slot]
        i, f = number // FB, number % FB
        k, yy, xx = f // 16, (f % 16) // 4, f % 4
        p = jnp.where(k == 1, xx * 4 + yy, yy * 4 + xx)
        qpair = jnp.concatenate([pre[0, k, p], pre[1, k, p]], axis=0)
        part = dot(xt[i], qpair)
        live = jnp.where(slot < counts[0, 0], 1.0, 0.0)
        gup_ref[0, 0, s] = (part * live).astype(BF16)
        return carry

    def activate(n, k):
        (activate_h, activate_q)[n](k)

    def wait_tokens(n, k):
        for copy in (got_x, got_g)[n]:
            copy.wait_recv()
        (load_up, load_dn)[n].wait()
        if n == 0:
            to_scalars.wait()

    def swap_tokens(n, k):
        held = (xs, gs)[n]
        got_d["xg"[n]] = remote(held.at[0], held.at[1], ssem_d.at[2, n], rsem_d.at[2, n], partner)

    def turn(n, k):
        got_d["x"].wait_recv()
        got_d["g"].wait_recv()
        for i in range(WB):
            cols = slice(BLK * i, BLK * i + BLK)
            for half in range(2):
                xt[i, :, BLK * half : BLK * half + BLK] = xs[half, :, cols].T
                gt[i, half] = gs[half, :, cols]

    got_z = {}

    def scatter_out(n, k):
        got_z[n] = scatter(n, (acc_o, acc_i)[n], (send_o, send_i)[n], (recv_o, recv_i)[n])

    def finish_sends(n, k):
        for copy in sends:
            copy.wait_send()
        sends.clear()

    def collect(n, k):
        gather_up(got_z[n], (acc_o, acc_i)[n], (recv_o, recv_i)[n], (out_ref, gin_ref)[n])

    def gradients(n, k):
        for j in range(CHUNKS):
            got_d[n, j].wait_recv()
        for part in range(3):
            lax.fori_loop(18 * part, 18 * part + 18, (grad_down, grad_up)[n], 0, unroll=18)

    steps = dict(
        w=wait_tokens, x=swap_tokens, m=make, f=forward, s=second, a=activate, d=spread, r=relay, u=use, t=turn, z=scatter_out, c=collect, e=finish_sends, g=gradients
    )
    for step in ORDER:
        steps[step[0]](int(step[1]), int(step[2]))


def write_out(*refs):
    copies = [pltpu.make_async_copy(refs[n], refs[n + 4], refs[8].at[n]) for n in range(4)]
    for copy in copies:
        copy.start()
    for copy in copies:
        copy.wait()


def on_device(inputs, up_blocks, down_blocks, slots, counts, grad_out):
    vmem = pl.BlockSpec(memory_space=pltpu.VMEM)
    anym = pl.BlockSpec(memory_space=pl.ANY)
    hbm = pl.BlockSpec(memory_space=pltpu.HBM)
    dma = pltpu.SemaphoreType.DMA
    scratch = [
        pltpu.SMEM((8, BLK), jnp.int32),
        pltpu.VMEM((8, BLK), jnp.int32),
        pltpu.SMEM((1, 1, CAP), jnp.int32),
        pltpu.VMEM((CAP + 1, BLK, BLK), BF16),
        pltpu.VMEM((CAP + 1, BLK, BLK), BF16),
        pltpu.VMEM((2, BLK, WB * BLK), BF16),
        pltpu.VMEM((2, BLK, WB * BLK), BF16),
        pltpu.VMEM((WB, BLK, 2 * BLK), BF16),
        pltpu.VMEM((WB, 2, BLK, BLK), BF16),
        pltpu.VMEM((CHUNKS, 4, BLK, BLK), BF16),
        pltpu.VMEM((CHUNKS, 4, BLK, BLK), BF16),
        pltpu.VMEM((CHUNKS, 2, 4, BLK, BLK), BF16),
        pltpu.VMEM((CHUNKS, 2, 4, BLK, BLK), BF16),
        pltpu.VMEM((CHUNKS, 8, BLK, BLK), F32),
        pltpu.VMEM((CHUNKS, 8, BLK, BLK), F32),
        pltpu.VMEM((CHUNKS, 2, 2, BLK, BLK), BF16),
        pltpu.VMEM((CHUNKS, 2, 2, BLK, BLK), BF16),
        pltpu.VMEM((CHUNKS, 2, 2, BLK, BLK), BF16),
        pltpu.VMEM((CHUNKS, 2, 2, BLK, BLK), BF16),
        pltpu.VMEM((CHUNKS, 3, 4, BLK, BLK), BF16),
        pltpu.VMEM((CHUNKS, 3, 4, BLK, BLK), BF16),
        pltpu.VMEM((CHUNKS, 4, BLK, BLK), BF16),
        pltpu.VMEM((CHUNKS, 4, BLK, BLK), BF16),
        pltpu.VMEM((CHUNKS, BLK, BLK), F32),
        pltpu.VMEM((CHUNKS, BLK, BLK), F32),
        pltpu.VMEM((CHUNKS, BLK, BLK), F32),
        pltpu.VMEM((CHUNKS, 3, BLK, BLK), BF16),
        pltpu.VMEM((CHUNKS, 3, BLK, BLK), BF16),
        pltpu.VMEM((2, CHUNKS, 16, BLK, BLK), BF16),
        pltpu.VMEM((2, CHUNKS, 16, BLK, BLK), BF16),
        pltpu.VMEM((BLK, WB * BLK), F32),
        pltpu.VMEM((BLK, WB * BLK), F32),
        pltpu.VMEM((BLK, WB * BLK), BF16),
        pltpu.VMEM((BLK, WB * BLK), BF16),
        pltpu.VMEM((NZ - 1, ROWS, WB * BLK), BF16),
        pltpu.VMEM((NZ - 1, ROWS, WB * BLK), BF16),
        dma((2,)),
        dma((2,)),
        dma((2, NZ)),
        dma((2, NZ)),
        dma((2, CHUNKS, 6)),
        dma((2, CHUNKS, 6)),
        dma((2, CHUNKS, 3)),
        dma((2, CHUNKS, 3)),
        dma((CHUNKS, 3)),
        dma((CHUNKS, 3)),
        dma((CHUNKS, 3)),
        dma((CHUNKS, 3)),
        dma((CHUNKS, 6)),
        dma((CHUNKS, 6)),
        dma((CHUNKS, 6)),
        dma((CHUNKS, 6)),
        dma((3, CHUNKS)),
        dma((3, CHUNKS)),
        dma((2, NZ - 1)),
        dma((2, NZ - 1)),
        dma((2,)),
    ]
    held = [pltpu.with_memory_space_constraint(a, pltpu.HBM) for a in (slots, inputs, grad_out, up_blocks, down_blocks)]
    shapes = (
        jax.ShapeDtypeStruct((ROWS, WB * BLK), BF16),
        jax.ShapeDtypeStruct((ROWS, WB * BLK), BF16),
        jax.ShapeDtypeStruct((1, 1, HALF, BLK, BLK), BF16),
        jax.ShapeDtypeStruct((1, 1, HALF, BLK, BLK), BF16),
    )
    results = pl.pallas_call(
        kernel,
        out_shape=shapes,
        in_specs=[hbm, pl.BlockSpec(memory_space=pltpu.SMEM)] + [hbm] * 4,
        out_specs=(vmem,) * 4,
        scratch_shapes=scratch,
        compiler_params=pltpu.CompilerParams(
            collective_id=0, has_side_effects=True, vmem_limit_bytes=48 * 1024 * 1024
        ),
    )(held[0], counts, *held[1:])
    return pl.pallas_call(
        write_out, out_shape=shapes, in_specs=[anym] * 4, out_specs=(hbm,) * 4, scratch_shapes=[dma((4,))],
        compiler_params=pltpu.CompilerParams(vmem_limit_bytes=4 * 1024 * 1024),
    )(*results)


def solution(mesh):
    return jax.shard_map(
        on_device,
        mesh=mesh,
        in_specs=(
            P(("depth", "col"), "row"),
            P("row", "col", None, None, None),
            P("row", "col", None, None, None),
            P("row", "col", None),
            P("row", "col"),
            P(("depth", "col"), "row"),
        ),
        out_specs=(
            P(("depth", "col"), "row"),
            P(("depth", "col"), "row"),
            P("row", "col", "depth", None, None),
            P("row", "col", "depth", None, None),
        ),
        check_vma=False,
    )
```

```python
import jax
import jax.numpy as jnp
from jax import lax
from jax.experimental import pallas as pl
from jax.experimental.pallas import tpu as pltpu
from jax.sharding import PartitionSpec as P

MESH = pl.DeviceIdType.MESH
F32, BF16 = jnp.float32, jnp.bfloat16
BLK, CAP, HALF = 128, 108, 54
WB, FB = 6, 48
NX, NY, NZ = 4, 4, 8
CHUNKS = 3
ROWS = 16
ORDER = (
    "w00m00m01m02w10m10m11f00f01m12f02f10f11s00s01s02f12x00x10s10",
    "s11a00a01s12a02t00a10d00d01a11a12d02d10r00r01d11d12r02r10u00",
    "r11u01r12u02z00u10u11v12u12z10g00c00g10e00c10",
)
LAST = (1, 2)
ORDER = [part[i : i + 3] for part in ORDER for i in range(0, len(part), 3)]

root_coeff = 0.7978845608
cube_coeff = 0.044715


def gelu_parts(preact):
    cubed = preact * preact * preact
    tangent = jnp.tanh(root_coeff * (preact + cube_coeff * cubed))
    values = 0.5 * preact * (1.0 + tangent)
    slopes = 0.5 * (1.0 + tangent) + 0.5 * preact * (1.0 - tangent * tangent) * root_coeff * (
        1.0 + 3.0 * cube_coeff * preact * preact
    )
    return (values, slopes)


def dot(a, b):
    return lax.dot_general(a, b, (((1,), (0,)), ((), ())), preferred_element_type=F32)


def dot_t(a, b):
    return lax.dot_general(a, b, (((1,), (1,)), ((), ())), preferred_element_type=F32)


def quad(a, b, c, d):
    return jnp.concatenate(
        [jnp.concatenate([a, b], axis=1), jnp.concatenate([c, d], axis=1)], axis=0
    )


def kernel(
    slots_in, counts, x_in, g_in, up_in, dn_in,
    out_ref, gin_ref, gup_ref, gdn_ref,
    inv, places, slots, up, dn, xs, gs, xt, gt, farp, farg, nearp, nearg, keptp, keptg, thrup, thrug, joinp, joing, r1p, r1g, s2p, s2g, ownp, owng, slopes, r2p, r2g,
    hid, pre, acc_o, acc_i, send_o, send_i, recv_o, recv_i,
    wsem, lsem, ssem_a, rsem_a, ssem_1, rsem_1, ssem_2, rsem_2, ssem_h, rsem_h, ssem_q, rsem_q, ssem_h4, rsem_h4, ssem_q4, rsem_q4,
    ssem_d, rsem_d, ssem_z, rsem_z, tsem,
):
    d, r, c = lax.axis_index("depth"), lax.axis_index("row"), lax.axis_index("col")
    y, x = r // NX, r % NX
    sends = []

    def at_x(o):
        return (d, y * NX + (x + o) % NX, c)

    def at_y(o):
        return (d, ((y + o) % NY) * NX + x, c)

    def at_z(o):
        return (d, r, (c + o) % NZ)

    partner = (1 - d, r, c)

    def remote(src, dst, ssem, rsem, device):
        copy = pltpu.make_async_remote_copy(
            src_ref=src, dst_ref=dst, send_sem=ssem, recv_sem=rsem, device_id=device, device_id_type=MESH
        )
        copy.start()
        sends.append(copy)
        return copy

    load_up = pltpu.make_async_copy(up_in.at[0, 0], up.at[pl.ds(0, CAP)], wsem.at[0])
    load_dn = pltpu.make_async_copy(dn_in.at[0, 0], dn.at[pl.ds(0, CAP)], wsem.at[1])
    mine = pl.ds(pl.multiple_of(c * ROWS, ROWS), ROWS)
    load_x = pltpu.make_async_copy(x_in, xs.at[0, mine], lsem.at[0])
    load_g = pltpu.make_async_copy(g_in, gs.at[0, mine], lsem.at[1])
    load_slots = pltpu.make_async_copy(slots_in, slots, tsem.at[0])
    load_slots.start()
    load_x.start()
    load_g.start()
    load_up.start()
    load_dn.start()
    up[CAP] = jnp.zeros((BLK, BLK), BF16)
    dn[CAP] = jnp.zeros((BLK, BLK), BF16)

    barrier = pltpu.get_barrier_semaphore()
    peers = [at_x(o) for o in (1, 2, 3)] + [at_y(o) for o in (1, 2, 3)]
    peers += [at_z(o) for o in range(1, NZ)] + [partner]
    for peer in peers:
        pl.semaphore_signal(barrier, inc=1, device_id=peer, device_id_type=MESH)
    pl.semaphore_wait(barrier, len(peers))

    got_x, got_g = [], []
    for n, (load, held, got) in enumerate(((load_x, xs, got_x), (load_g, gs, got_g))):
        load.wait()
        spot = held.at[0, mine]
        for o in (4, 3, 5, 2, 6, 1, 7):
            got.append(remote(spot, spot, ssem_a.at[n, o], rsem_a.at[n, o], at_z(o)))

    load_slots.wait()
    tile = (8, BLK)
    row, lane = lax.broadcasted_iota(jnp.int32, tile, 0), lax.broadcasted_iota(jnp.int32, tile, 1)
    number = jnp.where(lane < FB, row * FB + lane, WB * FB + BLK)

    def enter(slot, table):
        wanted = jnp.where(slot < counts[0, 0], slots[0, 0, slot], -1)
        return jnp.where(number == wanted, slot, table)

    places[...] = lax.fori_loop(0, CAP, enter, jnp.full(tile, CAP, jnp.int32), unroll=12)
    to_scalars = pltpu.make_async_copy(places, inv, tsem.at[1])
    to_scalars.start()

    def block(weights, i, f):
        return weights[inv[i, f]]

    def pair_p(fa, fb):
        acc = None
        for kk in range(3):
            w = quad(block(up, 2 * kk, fa), block(up, 2 * kk, fb), block(up, 2 * kk + 1, fa), block(up, 2 * kk + 1, fb))
            term = dot(xs[0, :, 256 * kk : 256 * kk + 256], w)
            acc = term if acc is None else acc + term
        return acc

    def pair_g(fa, fb):
        acc = None
        for kk in range(3):
            w = quad(block(dn, 2 * kk, fa), block(dn, 2 * kk + 1, fa), block(dn, 2 * kk, fb), block(dn, 2 * kk + 1, fb))
            term = dot_t(gs[0, :, 256 * kk : 256 * kk + 256], w)
            acc = term if acc is None else acc + term
        return acc

    far, near_out, kept, through, joined = (farp, farg), (nearp, nearg), (keptp, keptg), (thrup, thrug), (joinp, joing)
    first_in, second_out, own, second_in = (r1p, r1g), (s2p, s2g), (ownp, owng), (r2p, r2g)
    gathered, gsem, gsem4 = (hid, pre), ((ssem_h, rsem_h), (ssem_q, rsem_q)), ((ssem_h4, rsem_h4), (ssem_q4, rsem_q4))
    got_1, got_2, got_3, got_4, got_d = {}, {}, {}, {}, {}

    def x_first(n, k):
        return (n + k) % 2 == 0

    def axes(n, k):
        return (x, at_x, y, at_y) if x_first(n, k) else (y, at_y, x, at_x)

    def hidden_block(n, k, a, b):
        return 16 * k + (4 * b + a if x_first(n, k) else 4 * a + b)

    def send_1(n, k, i, src, dst, at):
        got_1[n, k, i] = remote(src, dst, ssem_1.at[n, k, i], rsem_1.at[n, k, i], at(3 if i % 2 else 1))

    def make(n, k):
        here, at, _, _ = axes(n, k)

        def product(o, m):
            a = (here + o) % 4
            return (pair_p, pair_g)[n](hidden_block(n, k, a, 2 * m), hidden_block(n, k, a, 2 * m + 1))

        def keep(ref, where, value):
            ref[where] = value[:, :BLK].astype(ref.dtype)
            ref[(*where[:-1], where[-1] + 1)] = value[:, BLK:].astype(ref.dtype)

        for m in range(2):
            keep(far[n], (k, 2 * m), product(2, m))
            send_1(n, k, m, far[n].at[k, pl.ds(2 * m, 2)], through[n].at[k, m], at)
        for way, o in ((0, 1), (1, 3)):
            keep(near_out[n], (k, way, 0), product(o, 1 - way))
            send_1(n, k, 2 + way, near_out[n].at[k, way, pl.ds(0, 2)], first_in[n].at[k, 1 + way, pl.ds(2 - 2 * way, 2)], at)
        for way, o in ((0, 1), (1, 3)):
            keep(kept[n], (k, 4 + 2 * way), product(o, way))
        for m in range(2):
            keep(kept[n], (k, 2 * m), product(0, m))

    def forward(n, k):
        _, at, _, _ = axes(n, k)
        for way in range(2):
            got_1[n, k, way].wait_recv()
            for i in range(2):
                total = kept[n][k, 4 + 2 * way + i] + through[n][k, way, i].astype(F32)
                joined[n][k, way, i] = total.astype(BF16)
            send_1(n, k, 4 + way, joined[n].at[k, way], first_in[n].at[k, 1 + way, pl.ds(2 * way, 2)], at)

    def second(n, k):
        _, _, here, at = axes(n, k)
        for i in range(2, 6):
            got_1[n, k, i].wait_recv()
        for o in (2, 1, 3, 0):
            b = (here + o) % 4
            total = kept[n][k, b]
            for i in range(1, 3):
                total = total + first_in[n][k, i, b].astype(F32)
            if o:
                second_out[n][k, b] = total.astype(BF16)
                got_2[n, k, o] = remote(
                    second_out[n].at[k, b], second_in[n].at[k, o - 1], ssem_2.at[n, k, o - 1], rsem_2.at[n, k, o - 1], at(o)
                )
            else:
                own[n][k] = total

    def summed(n, k):
        for o in (1, 2, 3):
            got_2[n, k, o].wait_recv()
        total = own[n][k]
        for j in range(3):
            total = total + second_in[n][k, j].astype(F32)
        return total

    def hand_out(n, k, share):
        a, _, b, at = axes(n, k)
        spot = gathered[n].at[0, k, a * 4 + b]
        gathered[n][0, k, a * 4 + b] = share.astype(BF16)
        for o in (2, 1, 3):
            got_3[n, k, o] = remote(spot, spot, gsem[n][0].at[k, o - 1], gsem[n][1].at[k, o - 1], at(o))

    def activate_h(k):
        values, slope = gelu_parts(summed(0, k))
        slopes[k] = slope
        hand_out(0, k, values)

    def activate_q(k):
        hand_out(1, k, summed(1, k) * slopes[k])

    def send_4(n, k, i, first, at):
        spot = gathered[n].at[0, k, pl.ds(first, 2)]
        got_4[n, k, i] = remote(spot, spot, gsem4[n][0].at[k, i], gsem4[n][1].at[k, i], at(3 if i % 2 else 1))

    def spread(n, k):
        a, at, _, _ = axes(n, k)
        for o in (1, 2, 3):
            got_3[n, k, o].wait_recv()
        for i, first in enumerate((0, 2, 2, 0)):
            send_4(n, k, i, a * 4 + first, at)

    def relay(n, k):
        a, at, _, _ = axes(n, k)
        for way, o in ((0, 3), (1, 1)):
            got_4[n, k, way].wait_recv()
            send_4(n, k, 4 + way, (a + o) % 4 * 4 + 2 * way, at)

    def multiply(n, k, first, places):
        weights, acc = ((dn, acc_o), (up, acc_i))[n]
        blocks = [hidden_block(n, k, a, b) for a, b in places]
        left = jnp.concatenate([gathered[n][0, k, a * 4 + b] for a, b in places], axis=1)
        for m in range(3):
            cols = slice(256 * m, 256 * m + 256)
            if n == 0:
                w = [jnp.concatenate([block(weights, 2 * m + u, f) for u in range(2)], axis=1) for f in blocks]
                part = dot(left, jnp.concatenate(w, axis=0))
            else:
                w = [jnp.concatenate([block(weights, 2 * m + u, f) for f in blocks], axis=1) for u in range(2)]
                part = dot_t(left, jnp.concatenate(w, axis=0))
            acc[:, cols] = part if first else acc[:, cols] + part

    def group(n, k, *offsets):
        here = axes(n, k)[0]
        return [((here + o) % 4, b) for o in offsets for b in range(4)]

    def use_near(n, k):
        for i in (2, 3):
            got_4[n, k, i].wait_recv()
        multiply(n, k, k == 0, group(n, k, 0, 1, 3))

    def use(n, k):
        split = (n, k) == LAST
        for i in (4, 5) if split else range(2, 6):
            got_4[n, k, i].wait_recv()
        got_d[n, k] = remote(gathered[n].at[0, k], gathered[n].at[1, k], ssem_d.at[n, k], rsem_d.at[n, k], partner)
        if split:
            multiply(n, k, False, group(n, k, 2))
        else:
            multiply(n, k, k == 0, [(p // 4, p % 4) for p in range(16)])

    def scatter(n, acc, buf, recv):
        got = []
        buf[...] = acc[...].astype(BF16)
        for o in (4, 3, 5, 2, 6, 1, 7):
            cc = (c + o) % NZ
            rows = pl.ds(pl.multiple_of(cc * ROWS, ROWS), ROWS)
            got.append(remote(buf.at[rows], recv.at[o - 1], ssem_z.at[n, o - 1], rsem_z.at[n, o - 1], at_z(o)))
        return got

    def gather_up(got, acc, recv, result):
        for copy in got:
            copy.wait_recv()
        total = acc[mine, :]
        for j in range(NZ - 1):
            total = total + recv[j].astype(F32)
        result[...] = total.astype(BF16)

    def grad_down(s, carry):
        slot = d * HALF + s
        number = slots[0, 0, slot]
        i, f = number // FB, number % FB
        k, yy, xx = f // 16, (f % 16) // 4, f % 4
        p = jnp.where(k == 1, yy * 4 + xx, xx * 4 + yy)
        hpair = jnp.concatenate([hid[0, k, p], hid[1, k, p]], axis=0)
        gpair = jnp.concatenate([gt[i, 0], gt[i, 1]], axis=0)
        part = lax.dot_general(hpair, gpair, (((0,), (0,)), ((), ())), preferred_element_type=F32)
        live = jnp.where(slot < counts[0, 0], 1.0, 0.0)
        gdn_ref[0, 0, s] = (part * live).astype(BF16)
        return carry

    def grad_up(s, carry):
        slot = d * HALF + s
        number = slots[0, 0, slot]
        i, f = number // FB, number % FB
        k, yy, xx = f // 16, (f % 16) // 4, f % 4
        p = jnp.where(k == 1, xx * 4 + yy, yy * 4 + xx)
        qpair = jnp.concatenate([pre[0, k, p], pre[1, k, p]], axis=0)
        part = dot(xt[i], qpair)
        live = jnp.where(slot < counts[0, 0], 1.0, 0.0)
        gup_ref[0, 0, s] = (part * live).astype(BF16)
        return carry

    def activate(n, k):
        (activate_h, activate_q)[n](k)

    def wait_tokens(n, k):
        for copy in (got_x, got_g)[n]:
            copy.wait_recv()
        (load_up, load_dn)[n].wait()
        if n == 0:
            to_scalars.wait()

    def swap_tokens(n, k):
        held = (xs, gs)[n]
        got_d["xg"[n]] = remote(held.at[0], held.at[1], ssem_d.at[2, n], rsem_d.at[2, n], partner)

    def turn(n, k):
        got_d["x"].wait_recv()
        got_d["g"].wait_recv()
        for i in range(WB):
            cols = slice(BLK * i, BLK * i + BLK)
            for half in range(2):
                xt[i, :, BLK * half : BLK * half + BLK] = xs[half, :, cols].T
                gt[i, half] = gs[half, :, cols]

    got_z = {}

    def scatter_out(n, k):
        got_z[n] = scatter(n, (acc_o, acc_i)[n], (send_o, send_i)[n], (recv_o, recv_i)[n])

    def finish_sends(n, k):
        for copy in sends:
            copy.wait_send()
        sends.clear()

    def collect(n, k):
        gather_up(got_z[n], (acc_o, acc_i)[n], (recv_o, recv_i)[n], (out_ref, gin_ref)[n])

    def gradients(n, k):
        for j in range(CHUNKS):
            got_d[n, j].wait_recv()
        for part in range(3):
            lax.fori_loop(18 * part, 18 * part + 18, (grad_down, grad_up)[n], 0, unroll=18)

    steps = dict(
        w=wait_tokens, x=swap_tokens, m=make, f=forward, s=second, a=activate, d=spread, r=relay, u=use, v=use_near, t=turn, z=scatter_out, c=collect, e=finish_sends, g=gradients
    )
    for step in ORDER:
        steps[step[0]](int(step[1]), int(step[2]))


def write_out(*refs):
    copies = [pltpu.make_async_copy(refs[n], refs[n + 4], refs[8].at[n]) for n in range(4)]
    for copy in copies:
        copy.start()
    for copy in copies:
        copy.wait()


def on_device(inputs, up_blocks, down_blocks, slots, counts, grad_out):
    vmem = pl.BlockSpec(memory_space=pltpu.VMEM)
    anym = pl.BlockSpec(memory_space=pl.ANY)
    hbm = pl.BlockSpec(memory_space=pltpu.HBM)
    dma = pltpu.SemaphoreType.DMA
    scratch = [
        pltpu.SMEM((8, BLK), jnp.int32),
        pltpu.VMEM((8, BLK), jnp.int32),
        pltpu.SMEM((1, 1, CAP), jnp.int32),
        pltpu.VMEM((CAP + 1, BLK, BLK), BF16),
        pltpu.VMEM((CAP + 1, BLK, BLK), BF16),
        pltpu.VMEM((2, BLK, WB * BLK), BF16),
        pltpu.VMEM((2, BLK, WB * BLK), BF16),
        pltpu.VMEM((WB, BLK, 2 * BLK), BF16),
        pltpu.VMEM((WB, 2, BLK, BLK), BF16),
        pltpu.VMEM((CHUNKS, 4, BLK, BLK), BF16),
        pltpu.VMEM((CHUNKS, 4, BLK, BLK), BF16),
        pltpu.VMEM((CHUNKS, 2, 4, BLK, BLK), BF16),
        pltpu.VMEM((CHUNKS, 2, 4, BLK, BLK), BF16),
        pltpu.VMEM((CHUNKS, 8, BLK, BLK), F32),
        pltpu.VMEM((CHUNKS, 8, BLK, BLK), F32),
        pltpu.VMEM((CHUNKS, 2, 2, BLK, BLK), BF16),
        pltpu.VMEM((CHUNKS, 2, 2, BLK, BLK), BF16),
        pltpu.VMEM((CHUNKS, 2, 2, BLK, BLK), BF16),
        pltpu.VMEM((CHUNKS, 2, 2, BLK, BLK), BF16),
        pltpu.VMEM((CHUNKS, 3, 4, BLK, BLK), BF16),
        pltpu.VMEM((CHUNKS, 3, 4, BLK, BLK), BF16),
        pltpu.VMEM((CHUNKS, 4, BLK, BLK), BF16),
        pltpu.VMEM((CHUNKS, 4, BLK, BLK), BF16),
        pltpu.VMEM((CHUNKS, BLK, BLK), F32),
        pltpu.VMEM((CHUNKS, BLK, BLK), F32),
        pltpu.VMEM((CHUNKS, BLK, BLK), F32),
        pltpu.VMEM((CHUNKS, 3, BLK, BLK), BF16),
        pltpu.VMEM((CHUNKS, 3, BLK, BLK), BF16),
        pltpu.VMEM((2, CHUNKS, 16, BLK, BLK), BF16),
        pltpu.VMEM((2, CHUNKS, 16, BLK, BLK), BF16),
        pltpu.VMEM((BLK, WB * BLK), F32),
        pltpu.VMEM((BLK, WB * BLK), F32),
        pltpu.VMEM((BLK, WB * BLK), BF16),
        pltpu.VMEM((BLK, WB * BLK), BF16),
        pltpu.VMEM((NZ - 1, ROWS, WB * BLK), BF16),
        pltpu.VMEM((NZ - 1, ROWS, WB * BLK), BF16),
        dma((2,)),
        dma((2,)),
        dma((2, NZ)),
        dma((2, NZ)),
        dma((2, CHUNKS, 6)),
        dma((2, CHUNKS, 6)),
        dma((2, CHUNKS, 3)),
        dma((2, CHUNKS, 3)),
        dma((CHUNKS, 3)),
        dma((CHUNKS, 3)),
        dma((CHUNKS, 3)),
        dma((CHUNKS, 3)),
        dma((CHUNKS, 6)),
        dma((CHUNKS, 6)),
        dma((CHUNKS, 6)),
        dma((CHUNKS, 6)),
        dma((3, CHUNKS)),
        dma((3, CHUNKS)),
        dma((2, NZ - 1)),
        dma((2, NZ - 1)),
        dma((2,)),
    ]
    held = [pltpu.with_memory_space_constraint(a, pltpu.HBM) for a in (slots, inputs, grad_out, up_blocks, down_blocks)]
    shapes = (
        jax.ShapeDtypeStruct((ROWS, WB * BLK), BF16),
        jax.ShapeDtypeStruct((ROWS, WB * BLK), BF16),
        jax.ShapeDtypeStruct((1, 1, HALF, BLK, BLK), BF16),
        jax.ShapeDtypeStruct((1, 1, HALF, BLK, BLK), BF16),
    )
    results = pl.pallas_call(
        kernel,
        out_shape=shapes,
        in_specs=[hbm, pl.BlockSpec(memory_space=pltpu.SMEM)] + [hbm] * 4,
        out_specs=(vmem,) * 4,
        scratch_shapes=scratch,
        compiler_params=pltpu.CompilerParams(
            collective_id=0, has_side_effects=True, vmem_limit_bytes=48 * 1024 * 1024
        ),
    )(held[0], counts, *held[1:])
    return pl.pallas_call(
        write_out, out_shape=shapes, in_specs=[anym] * 4, out_specs=(hbm,) * 4, scratch_shapes=[dma((4,))],
        compiler_params=pltpu.CompilerParams(vmem_limit_bytes=4 * 1024 * 1024),
    )(*results)


def solution(mesh):
    return jax.shard_map(
        on_device,
        mesh=mesh,
        in_specs=(
            P(("depth", "col"), "row"),
            P("row", "col", None, None, None),
            P("row", "col", None, None, None),
            P("row", "col", None),
            P("row", "col"),
            P(("depth", "col"), "row"),
        ),
        out_specs=(
            P(("depth", "col"), "row"),
            P(("depth", "col"), "row"),
            P("row", "col", "depth", None, None),
            P("row", "col", "depth", None, None),
        ),
        check_vma=False,
    )
```
